32 devices in a mesh: tm: 8 (over z, y), space: 4 (over x, core).
Axes of the slice: x: 2, y: 2, z: 4, core: 2. Of those that a mesh axis runs over, the one named last changes fastest.
Arguments:
- inverse_factor: bfloat16 [2, 8, 4096, 4096], P(None, 'tm', 'space'), may hold values from -1.5 to 1.5, as said below
- tile_mask: int32 [32, 32], replicated, may hold values 0 or 1
- carry_rate: float32 [8, 4096, 2], P('tm', 'space'), may hold values from 0 to 1
- right_side: float32 [8, 4096, 2, 128], P('tm', 'space'), may hold values from -1.5 to 1.5
- arrow_rows: bfloat16 [8, 4096, 2, 512], P('tm', 'space'), may hold values from -0.125 to 0.125
- fixed_rhs: float32 [2, 512, 128], P(None, ('tm', 'space')), may hold values from -6 to 6
- tip_factor: bfloat16 [2, 512, 512], replicated, may hold values from -1 to 1, as said below
Outputs:
- solution: float32 [8, 4096, 2, 128], P('tm', 'space')
- fixed_solution: float32 [2, 512, 128], P(None, ('tm', 'space'))
The draws below stay inside these ranges and needn't reach their ends.
Inputs may be any that keep to these rules, and one draw needn't show every extreme that they name: `tile_mask`: 1 marks a tile that may be nonzero. `inverse_factor`: only entries on or below the diagonal are read. `tip_factor`: only entries on or below the diagonal are read.
All inputs are finite; a program needn't handle non-finite values.
Results may differ from the reference program's by a relative error of at most 0.022.
Values may be sent and summed in bfloat16 or wider, within the bound.
A program may use at most 320 MiB of HBM per device.

```python
import math
import jax
import jax.numpy as jnp
from jax import lax

SPATIAL_NODES = 4096
TILE = 128
F = 512
HYPER_SETTINGS = 2
K = 128
TIMES = 8
TILES = 32


def draw_carry_rate(key, part):
    split_keys = jax.random.split(key, 6)
    slow_share = 0.5
    slow_nodes = jax.random.uniform(split_keys[0], (1, SPATIAL_NODES, HYPER_SETTINGS)) < slow_share
    kept_share = jax.random.uniform(split_keys[1], (1, SPATIAL_NODES, HYPER_SETTINGS), minval=0.25, maxval=0.6)
    jitter = jax.random.uniform(split_keys[2], (TIMES, SPATIAL_NODES, HYPER_SETTINGS), minval=0.5, maxval=1.5)
    gradual_rate = jnp.exp(jnp.log(kept_share) * jitter / TIMES)
    place_indices = jax.random.randint(split_keys[3], (2, 1, 1, HYPER_SETTINGS), 1, TIMES)
    temporal_index = jnp.arange(TIMES)[None, :, None, None]
    sudden_rows = jnp.any(place_indices == temporal_index, axis=0)
    sudden_loss = jax.random.uniform(split_keys[4], (1, SPATIAL_NODES, HYPER_SETTINGS), minval=0.65, maxval=0.8)
    fast_rate = jax.random.uniform(split_keys[5], (TIMES, SPATIAL_NODES, HYPER_SETTINGS), minval=0.1, maxval=0.6)
    gradual_portion = gradual_rate * jnp.where(sudden_rows, sudden_loss, 1.0)
    return jnp.where(slow_nodes, gradual_portion, fast_rate).astype(jnp.float32)


def triangular_block(block_key, order, diag_low, diag_high, spread):
    noise_key, diag_key = jax.random.split(block_key)
    noise_vals = jnp.clip(jax.random.normal(noise_key, (order, order)), -5.0, 5.0)
    diagonal = jax.random.uniform(diag_key, (order, 1), minval=diag_low, maxval=diag_high)
    place_indices = jnp.arange(order)
    on_diagonal = place_indices[:, None] == place_indices[None, :]
    return jnp.where(on_diagonal, diagonal, noise_vals * (spread / math.sqrt(order))).astype(jnp.bfloat16)


def draw_inverse_factor(key, part):

    def one_block(block_index):
        return triangular_block(jax.random.fold_in(key, block_index), SPATIAL_NODES, 0.6, 1.4, 1.2)
    blocks = lax.map(one_block, jnp.arange(HYPER_SETTINGS * TIMES))
    return blocks.reshape(HYPER_SETTINGS, TIMES, SPATIAL_NODES, SPATIAL_NODES)


def draw_tip_factor(key, part):

    def one_block(block_index):
        return triangular_block(jax.random.fold_in(key, block_index + 7919), F, 0.35, 0.7, 0.5)
    return lax.map(one_block, jnp.arange(HYPER_SETTINGS))


def with_ends(array, rng, smallest, largest):
    longest = array.shape.index(max(array.shape))
    spots = []
    for shift in (0, 1):
        where = [jax.random.randint(jax.random.fold_in(rng, axis), (), 0, length) for axis, length in enumerate(array.shape)]
        where[longest] = (where[longest] + shift) % array.shape[longest]
        spots.append(tuple(where))
    return array.at[spots[0]].set(smallest).at[spots[1]].set(largest)


def level_of(stream_key, shape, pieces, least, high):
    loudness, own = 1.0, jax.random.fold_in(stream_key, 6)
    for axis_at, parts in pieces:
        draws = jnp.exp(jax.random.uniform(jax.random.fold_in(own, axis_at), (parts,), jnp.float32, least / len(pieces), high / len(pieces)))
        loudness = loudness * jnp.repeat(draws, shape[axis_at] // parts).reshape([-1 if axis == axis_at else 1 for axis in range(len(shape))])
    return loudness


def scatter_about(own_key, dims, deviation, bound, shards=(), kind=jnp.bfloat16):
    result = deviation * jax.random.normal(own_key, dims, jnp.float32)
    if shards:
        result = result * level_of(own_key, dims, shards, -0.22, 0.18)
    return jnp.clip(result, -bound, bound).astype(kind)


def setup_inputs(seed: int = 0) -> dict:
    key_of = jax.random.split(jax.random.key(seed), 8)
    inverse_factor = draw_inverse_factor(jax.random.fold_in(key_of[7], 71), 0)
    tile_mask = with_ends((jax.random.randint(key_of[1], (TILES, TILES), 0, 2) < 1).astype(jnp.int32), jax.random.fold_in(key_of[1], 1), 0, 1)
    carry_rate = draw_carry_rate(jax.random.fold_in(key_of[7], 71), 0)
    right_side = scatter_about(key_of[3], (TIMES, SPATIAL_NODES, HYPER_SETTINGS, K), 0.25, 1.5, ((0, 8), (1, 4)), jnp.float32)
    arrow_rows = scatter_about(key_of[4], (TIMES, SPATIAL_NODES, HYPER_SETTINGS, F), (4.0 * (TIMES * SPATIAL_NODES) ** -0.5), 0.125, ((0, 8), (1, 4)))
    fixed_rhs = scatter_about(key_of[5], (HYPER_SETTINGS, F, K), 1.0, 6.0, ((1, 32),), jnp.float32)
    tip_factor = draw_tip_factor(jax.random.fold_in(key_of[7], 71), 0)
    return {"inverse_factor": inverse_factor, "tile_mask": tile_mask, "carry_rate": carry_rate, "right_side": right_side, "arrow_rows": arrow_rows, "fixed_rhs": fixed_rhs, "tip_factor": tip_factor}


def kept_cells(tile_mask):
    tile_count = tile_mask.shape[0]
    marked = jnp.maximum(tile_mask, jnp.eye(tile_count, dtype=jnp.int32))
    expanded = jnp.repeat(jnp.repeat(marked, TILE, axis=0), TILE, axis=1)
    place_indices = jnp.arange(SPATIAL_NODES, dtype=jnp.int32)
    return (expanded > 0) & (place_indices[:, None] >= place_indices[None, :])


def reference(inverse_factor, tile_mask, carry_rate, right_side, arrow_rows, fixed_rhs, tip_factor):
    highest = lax.Precision.HIGHEST
    kept = kept_cells(tile_mask)

    def forward_step(carried_value, inputs):
        rate_now, source = inputs
        current = source + rate_now[:, :, None] * carried_value
        return current, current

    _, forward = lax.scan(forward_step, jnp.zeros((SPATIAL_NODES, HYPER_SETTINGS, K), jnp.float32), (carry_rate, right_side))
    forward_b = lax.optimization_barrier(forward.astype(jnp.bfloat16))

    def block_step(block_index):
        factor = lax.dynamic_index_in_dim(inverse_factor, block_index, 1, keepdims=False)
        factor = jnp.where(kept[None], factor, jnp.zeros((), jnp.bfloat16)).astype(jnp.float32)
        vector = lax.dynamic_index_in_dim(forward_b, block_index, 0, keepdims=False).astype(jnp.float32)
        inner_rows = jnp.einsum('hij,jhk->ihk', factor, vector, precision=highest).astype(jnp.bfloat16)
        inner_rows = lax.optimization_barrier(inner_rows).astype(jnp.float32)
        scaled = jnp.einsum('hij,ihk->jhk', factor, inner_rows, precision=highest)
        arrow_part = lax.dynamic_index_in_dim(arrow_rows, block_index, 0, keepdims=False).astype(jnp.float32)
        coupling = jnp.einsum('shf,shk->hfk', arrow_part, vector, precision=highest)
        return scaled, coupling

    scaled, coupling = lax.map(block_step, jnp.arange(TIMES, dtype=jnp.int32))
    fixed_forward = (fixed_rhs - jnp.sum(coupling, axis=0)).astype(jnp.bfloat16)
    fixed_forward = lax.optimization_barrier(fixed_forward).astype(jnp.float32)
    fixed_index = jnp.arange(F, dtype=jnp.int32)
    lower_tri = fixed_index[:, None] >= fixed_index[None, :]
    tip_lower = jnp.where(lower_tri[None], tip_factor, jnp.zeros((), jnp.bfloat16)).astype(jnp.float32)
    tip_inner = jnp.einsum('hij,hjk->hik', tip_lower, fixed_forward, precision=highest).astype(jnp.bfloat16)
    tip_inner = lax.optimization_barrier(tip_inner).astype(jnp.float32)
    fixed_solution = jnp.einsum('hij,hik->hjk', tip_lower, tip_inner, precision=highest)
    fixed_b = lax.optimization_barrier(fixed_solution.astype(jnp.bfloat16)).astype(jnp.float32)

    def carried_step(block_index):
        arrow_part = lax.dynamic_index_in_dim(arrow_rows, block_index, 0, keepdims=False).astype(jnp.float32)
        scaled_now = lax.dynamic_index_in_dim(scaled, block_index, 0, keepdims=False)
        return scaled_now - jnp.einsum('shf,hfk->shk', arrow_part, fixed_b, precision=highest)

    carried = lax.map(carried_step, jnp.arange(TIMES, dtype=jnp.int32))

    def backward_step(passed, inputs):
        rate_now, carried_now = inputs
        current = carried_now + passed
        return rate_now[:, :, None] * current, current

    _, solution = lax.scan(backward_step, jnp.zeros((SPATIAL_NODES, HYPER_SETTINGS, K), jnp.float32), (carry_rate, carried), reverse=True)
    return solution, fixed_solution
```

```python
import functools

import jax
import jax.numpy as jnp
from jax import lax
from jax.experimental import pallas as pl
from jax.experimental.pallas import tpu as pltpu
from jax.sharding import PartitionSpec as P

TILE = 128
CHUNKS = 4
H = 2
CORES = 2
LAG = 2
F32 = jnp.float32
BF16 = jnp.bfloat16


def turned(a):
    return a.astype(F32).T


def kernel(
    times, spaces,
    weights, keep, rate, source, arrow, rhs, tip,
    out, fixed_out,
    w_v, keep_v, rate_v, rate_p, src_v, arrow_v, rhs_v, tip_v, sol_v, fix_v,
    r_v, s_out, s_in, ch_out, ch_in, f_all,
    c_f, c_out, c_in1, c_part, c_in2, ff, fixed_b,
    inner, inner_t, own_part, sib_out, sib_in, red_out, red_in,
    carr, b_out, b_in, bc_out, bc_in,
    local_sem, w_sem, rate_sem, pair_s, pair_r, ch_s, ch_r,
    x_s, sib_s, f_r, c1_s, c1_r, c2_s, c2_r, c3_s, c3_r,
    sp_s, sp_r, rd_s, rd_r, bp_s, bp_r, bc_s, bc_r, out_sem,
):
    rows = f_all.shape[2]
    step_rows = rows // CHUNKS
    fixed_total = ff.shape[1]
    share = fixed_total // times
    xs = spaces // CORES
    t = lax.axis_index("tm")
    p = lax.axis_index("space")
    x = p // CORES
    c = p % CORES
    y = t % 2
    z = t // 2
    z_total = times // 2
    partner = t + 1 - 2 * y
    sibling = p + 1 - 2 * c

    def remote(src, dst, send, recv, tm, space):
        return pltpu.make_async_remote_copy(
            src_ref=src, dst_ref=dst, send_sem=send, recv_sem=recv,
            device_id={"tm": tm, "space": space}, device_id_type=pl.DeviceIdType.MESH,
        )

    loads = [
        pltpu.make_async_copy(a, b, local_sem.at[i])
        for i, (a, b) in enumerate(
            ((source, src_v), (rate, rate_v), (keep, keep_v), (rhs, rhs_v), (tip, tip_v), (arrow, arrow_v))
        )
    ]
    for load in loads:
        load.start()

    def w_copy(h, q):
        cols = pl.ds(pl.multiple_of(q * rows, rows), rows)
        return pltpu.make_async_copy(weights.at[h, :, cols], w_v.at[h, :, cols], w_sem.at[h, q])

    barrier = pltpu.get_barrier_semaphore()

    def greet_t(d, _):
        pl.semaphore_signal(
            barrier, inc=1, device_id={"tm": (t + d) % times, "space": p},
            device_id_type=pl.DeviceIdType.MESH,
        )
        return 0

    def greet_s(d, _):
        pl.semaphore_signal(
            barrier, inc=1, device_id={"tm": t, "space": (p + d) % spaces},
            device_id_type=pl.DeviceIdType.MESH,
        )
        return 0

    lax.fori_loop(1, times, greet_t, 0)
    lax.fori_loop(1, spaces, greet_s, 0)
    for h in range(H):
        lax.fori_loop(0, p + 1, lambda q, _, h=h: (w_copy(h, q).start(), 0)[1], 0)
    loads[0].wait()
    loads[1].wait()

    def part(k):
        return pl.ds(pl.multiple_of(k * step_rows, step_rows), step_rows)

    def woven(h, k):
        return pl.ds(2 * k * step_rows + h, step_rows, stride=2)

    for h in range(H):
        for k in range(CHUNKS):
            s_out[h, part(k)] = src_v[woven(h, k), :].astype(BF16)
    pl.semaphore_wait(barrier, times - 1 + spaces - 1)

    def pair_copy(h, k):
        i = h * CHUNKS + k
        return remote(s_out.at[h, part(k)], s_in.at[h, part(k)], pair_s.at[i], pair_r.at[i], partner, p)

    rate_copy = remote(rate_v, rate_p, rate_sem.at[0], rate_sem.at[1], partner, p)
    rate_copy.start()
    for h in range(H):
        for k in range(CHUNKS):
            pair_copy(h, k).start()

    tiles = rows // TILE

    def spread(ref, parity):
        for h in range(H):
            for j in range(tiles):
                row = ref[pl.ds(h * tiles + j, 1), :]
                r_v[parity, h, pl.ds(j * TILE, TILE), :] = jnp.broadcast_to(row, (TILE, TILE)).T

    spread(rate_v, y)

    @pl.when(z == 0)
    def _():
        ch_in[...] = jnp.zeros_like(ch_in)

    @pl.when(z == z_total - 1)
    def _():
        bc_in[...] = jnp.zeros_like(bc_in)

    rate_copy.wait_recv()
    spread(rate_p, 1 - y)

    def chain_copy(h, k):
        i = h * CHUNKS + k
        return remote(
            ch_out.at[h, part(k)], ch_in.at[h, part(k)], ch_s.at[i], ch_r.at[i], (t + 2) % times, p
        )

    def x_copy(h, k, other):
        i = h * CHUNKS + k
        piece = f_all.at[h, p, part(k)]
        return remote(piece, piece, x_s.at[i, other], f_r.at[i, p], t, other * CORES + c)

    def sib_copy(h, k, from_x):
        i = h * CHUNKS + k
        q = from_x * CORES + c
        piece = f_all.at[h, q, part(k)]
        return remote(piece, piece, sib_s.at[i, from_x], f_r.at[i, q], t, sibling)

    def got(h, k, q):
        i = h * CHUNKS + k
        piece = f_all.at[h, q, part(k)]
        return remote(piece, piece, sib_s.at[i, 0], f_r.at[i, q], t, sibling)

    def scan_chunk(h, k):
        pair_copy(h, k).wait_recv()

        @pl.when(z > 0)
        def _():
            chain_copy(h, k).wait_recv()

        mine = src_v[woven(h, k), :]
        theirs = s_in[h, part(k)].astype(F32)
        s_e = jnp.where(y == 0, mine, theirs)
        s_o = jnp.where(y == 0, theirs, mine)
        f_e = s_e + r_v[0, h, part(k)] * ch_in[h, part(k)].astype(F32)
        f_o = s_o + r_v[1, h, part(k)] * f_e
        ch_out[h, part(k)] = f_o.astype(BF16)

        @pl.when(z < z_total - 1)
        def _():
            chain_copy(h, k).start()

        f_all[h, p, part(k)] = jnp.where(y == 0, f_e, f_o).astype(BF16)
        lax.fori_loop(x + 1, xs, lambda o, _: (x_copy(h, k, o).start(), 0)[1], 0)

        @pl.when(c == 0)
        def _():
            sib_copy(h, k, x).start()

    def relay(h, k):
        def one(o, _):
            got(h, k, o * CORES + c).wait_recv()
            sib_copy(h, k, o).start()
            return 0

        lax.fori_loop(0, x, one, 0)

    def scan_step(i, _):
        @pl.when(i < H * CHUNKS)
        def _():
            scan_chunk(i // CHUNKS, i % CHUNKS)

        @pl.when(i >= LAG)
        def _():
            relay((i - LAG) // CHUNKS, (i - LAG) % CHUNKS)

        return 0

    lax.fori_loop(0, H * CHUNKS + LAG, scan_step, 0)

    def ds_share(n):
        return pl.ds(pl.multiple_of(n * share, share), share)

    def c1_copy(h, d):
        to = (t + d) % times
        return remote(
            c_out.at[h, ds_share(to)], c_in1.at[h, d], c1_s.at[h, d], c1_r.at[h, d], to, p
        )

    def c2_copy(h, d):
        return remote(
            c_part.at[h], c_in2.at[h, d], c2_s.at[h, d], c2_r.at[h, d], t, (p + d) % spaces
        )

    def c3_copy(h, d):
        return remote(
            ff.at[h, ds_share(t)], ff.at[h, ds_share(t)], c3_s.at[h, d], c3_r.at[h, d],
            (t + d) % times, p,
        )

    def c3_got(h, d):
        piece = ff.at[h, ds_share((t - d + times) % times)]
        return remote(piece, piece, c3_s.at[h, d], c3_r.at[h, d], (t + d) % times, p)

    loads[3].wait()
    loads[5].wait()
    for h in range(H):
        f_t = turned(f_all[h, p]).astype(BF16)
        coupling = jnp.dot(f_t, arrow_v[h], preferred_element_type=F32).T
        c_f[h] = rhs_v[h] - coupling
        c_out[h] = c_f[h].astype(BF16)
        lax.fori_loop(1, times, lambda d, _, h=h: (c1_copy(h, d).start(), 0)[1], 0)

    def second(h):
        def add(d, acc):
            c1_copy(h, d).wait_recv()
            return acc + c_in1[h, d].astype(F32)

        c_part[h] = lax.fori_loop(1, times, add, c_f[h, ds_share(t)])
        lax.fori_loop(1, spaces, lambda d, _: (c2_copy(h, d).start(), 0)[1], 0)

    def third(h):
        def add(d, acc):
            c2_copy(h, d).wait_recv()
            return acc + c_in2[h, d]

        ff[h, ds_share(t)] = lax.fori_loop(1, spaces, add, c_part[h]).astype(BF16)
        lax.fori_loop(1, times, lambda d, _: (c3_copy(h, d).start(), 0)[1], 0)

    def tip_solve(h):
        lax.fori_loop(1, times, lambda d, _: (c3_got(h, d).wait_recv(), 0)[1], 0)
        lower = lax.broadcasted_iota(jnp.int32, (fixed_total, fixed_total), 0) >= (
            lax.broadcasted_iota(jnp.int32, (fixed_total, fixed_total), 1)
        )
        tip_l = jnp.where(lower, tip_v[h], jnp.zeros((), BF16))
        tip_in = jnp.dot(tip_l, ff[h], preferred_element_type=F32).astype(BF16)
        fixed = jnp.dot(turned(tip_in).astype(BF16), tip_l, preferred_element_type=F32).T
        fix_v[h] = fixed
        fixed_b[h] = fixed.astype(BF16)

    block = 2 * TILE

    def masked(h, b, q):
        cols = pl.ds(pl.multiple_of(q * rows, rows), rows)
        pieces = []
        for j in range(block // TILE):
            at = pl.ds(pl.multiple_of(b * block + j * TILE, TILE), TILE)
            kept = keep_v[pl.ds(b * (block // TILE) + j, 1), cols].astype(BF16)
            pieces.append(w_v[h, at, cols] * kept)
        return jnp.concatenate(pieces, axis=0), cols

    def first_product(h):
        def wait_block(q, _):
            w_copy(h, q).wait()
            relayed = ((q % CORES) == c) & (q // CORES < x)

            @pl.when((q < p) & jnp.logical_not(relayed))
            def _():
                lax.fori_loop(0, CHUNKS, lambda k, _: (got(h, k, q).wait_recv(), 0)[1], 0)

            return 0

        lax.fori_loop(0, p + 1, wait_block, 0)

        def row_block(b, _):
            at = pl.ds(pl.multiple_of(b * block, block), block)

            def below(q, acc):
                piece, cols = masked(h, b, q)
                w_v[h, at, cols] = piece
                return acc + jnp.dot(piece, f_all[h, q], preferred_element_type=F32)

            acc = lax.fori_loop(0, p, below, jnp.zeros((block, f_all.shape[3]), F32))
            piece, cols = masked(h, b, p)
            row_id = b * block + lax.broadcasted_iota(jnp.int32, (block, rows), 0)
            col_id = lax.broadcasted_iota(jnp.int32, (block, rows), 1)
            piece = jnp.where(row_id >= col_id, piece, jnp.zeros((), BF16))
            w_v[h, at, cols] = piece
            acc = acc + jnp.dot(piece, f_all[h, p], preferred_element_type=F32)
            inner[h, at] = acc.astype(BF16)
            return 0

        lax.fori_loop(0, rows // block, row_block, 0)
        inner_t[h] = turned(inner[h]).astype(BF16)

    def back(h, q, put):
        def col_block(b, _):
            cols = pl.ds(pl.multiple_of(q * rows + b * block, block), block)
            value = jnp.dot(inner_t[h], w_v[h, :, cols], preferred_element_type=F32).T
            put(pl.ds(pl.multiple_of(b * block, block), block), value)
            return 0

        lax.fori_loop(0, rows // block, col_block, 0)

    def sp_copy(h, o):
        return remote(sib_out.at[h, o], sib_in.at[h, o], sp_s.at[h, o], sp_r.at[h, o], t, sibling)

    def rd_copy(h, o):
        return remote(
            red_out.at[h, o], red_in.at[h, x], rd_s.at[h, o], rd_r.at[h, x], t, o * CORES + c
        )

    def rd_got(h, o):
        return remote(red_out.at[h, o], red_in.at[h, o], rd_s.at[h, o], rd_r.at[h, o], t, sibling)

    def second_product(h):
        def for_sibling(o, _):
            def put(at, value):
                sib_out[h, o, at] = value.astype(BF16)

            back(h, o * CORES + 1 - c, put)
            sp_copy(h, o).start()
            return 0

        lax.fori_loop(0, x + c, for_sibling, 0)

        def for_own(o, _):
            def put(at, value):
                own_part[h, o, at] = value

            back(h, o * CORES + c, put)
            return 0

        lax.fori_loop(0, x + 1, for_own, 0)

    def pass_on(h):
        def one(o, _):
            sp_copy(h, o).wait_recv()
            red_out[h, o] = (own_part[h, o] + sib_in[h, o].astype(F32)).astype(BF16)
            rd_copy(h, o).start()
            return 0

        lax.fori_loop(0, x, one, 0)

    loads[2].wait()
    first_product(0)
    second_product(0)
    second(0)
    pass_on(0)
    second(1)
    first_product(1)
    third(0)
    second_product(1)
    third(1)
    pass_on(1)
    loads[4].wait()
    tip_solve(0)
    tip_solve(1)

    def bp_copy(h, k):
        i = h * CHUNKS + k
        return remote(b_out.at[h, part(k)], b_in.at[h, part(k)], bp_s.at[i], bp_r.at[i], partner, p)

    def bc_copy(h, k):
        i = h * CHUNKS + k
        return remote(
            bc_out.at[h, part(k)], bc_in.at[h, part(k)], bc_s.at[i], bc_r.at[i],
            (t + times - 2) % times, p,
        )

    def gather_scaled(h):
        @pl.when(c == 0)
        def _():
            sp_copy(h, x).wait_recv()

        lax.fori_loop(x + 1, xs, lambda o, _: (rd_got(h, o).wait_recv(), 0)[1], 0)

        def one(k, _):
            at = part(k)
            drop = jnp.dot(arrow_v[h, at], fixed_b[h], preferred_element_type=F32)
            carr[h, at] = own_part[h, x, at] - drop

            @pl.when(c == 0)
            def _():
                carr[h, at] += sib_in[h, x, at].astype(F32)

            def more(o, _):
                carr[h, at] += red_in[h, o, at].astype(F32)
                return 0

            lax.fori_loop(x + 1, xs, more, 0)
            b_out[h, at] = carr[h, at].astype(BF16)
            bp_copy(h, k).start()
            return 0

        lax.fori_loop(0, CHUNKS, one, 0)

    def back_chunk(h, k):
        bp_copy(h, k).wait_recv()

        @pl.when(z < z_total - 1)
        def _():
            bc_copy(h, k).wait_recv()

        mine = carr[h, part(k)]
        theirs = b_in[h, part(k)].astype(F32)
        c_e = jnp.where(y == 0, mine, theirs)
        c_o = jnp.where(y == 0, theirs, mine)
        sol_o = c_o + bc_in[h, part(k)].astype(F32)
        sol_e = c_e + r_v[1, h, part(k)] * sol_o
        bc_out[h, part(k)] = (r_v[0, h, part(k)] * sol_e).astype(BF16)

        @pl.when(z > 0)
        def _():
            bc_copy(h, k).start()

        sol_v[woven(h, k), :] = jnp.where(y == 0, sol_e, sol_o)

    gather_scaled(0)
    gather_scaled(1)
    lax.fori_loop(0, H * CHUNKS, lambda i, _: (back_chunk(i // CHUNKS, i % CHUNKS), 0)[1], 0)
    out_copy = pltpu.make_async_copy(sol_v, out, out_sem.at[0])
    fix_copy = pltpu.make_async_copy(fix_v, fixed_out, out_sem.at[1])
    out_copy.start()
    fix_copy.start()

    rate_copy.wait_send()

    def drain(i, _):
        h, k = i // CHUNKS, i % CHUNKS
        pair_copy(h, k).wait_send()
        bp_copy(h, k).wait_send()

        @pl.when(z < z_total - 1)
        def _():
            chain_copy(h, k).wait_send()

        @pl.when(z > 0)
        def _():
            bc_copy(h, k).wait_send()

        lax.fori_loop(x + 1, xs, lambda o, _: (x_copy(h, k, o).wait_send(), 0)[1], 0)
        lax.fori_loop(0, x + 1 - c, lambda o, _: (sib_copy(h, k, o).wait_send(), 0)[1], 0)
        return 0

    lax.fori_loop(0, H * CHUNKS, drain, 0)

    for h in range(H):
        lax.fori_loop(1, times, lambda d, _, h=h: (c1_copy(h, d).wait_send(), 0)[1], 0)
        lax.fori_loop(1, spaces, lambda d, _, h=h: (c2_copy(h, d).wait_send(), 0)[1], 0)
        lax.fori_loop(1, times, lambda d, _, h=h: (c3_copy(h, d).wait_send(), 0)[1], 0)
        lax.fori_loop(0, x + c, lambda o, _, h=h: (sp_copy(h, o).wait_send(), 0)[1], 0)
        lax.fori_loop(0, x, lambda o, _, h=h: (rd_copy(h, o).wait_send(), 0)[1], 0)
    out_copy.wait()
    fix_copy.wait()


def on_device(times, spaces, inverse_factor, tile_mask, carry_rate, right_side, arrow_rows, fixed_rhs, tip_factor):
    rows = right_side.shape[1]
    nodes = inverse_factor.shape[3]
    k = right_side.shape[3]
    fixed_total = tip_factor.shape[1]
    xs = spaces // CORES
    share = fixed_total // times
    tile_total = tile_mask.shape[0]
    own_tiles = rows // TILE
    table = jnp.maximum(tile_mask, jnp.eye(tile_total, dtype=jnp.int32))
    own = lax.dynamic_slice_in_dim(table, lax.axis_index("space") * own_tiles, own_tiles, 0)
    keep = jnp.repeat((own > 0).astype(F32), TILE, axis=1)
    rate = carry_rate[0].T.reshape(H * own_tiles, TILE)
    source = right_side.reshape(H * rows, k)
    arrow = arrow_rows[0].transpose(1, 0, 2)
    share_rows = fixed_rhs.shape[1]
    start = lax.axis_index(("tm", "space")) * share_rows
    rhs = lax.dynamic_update_slice_in_dim(
        jnp.zeros((H, fixed_total, k), F32), fixed_rhs, start, 1
    )
    weights = inverse_factor[:, 0]
    n = H * CHUNKS
    dma = pltpu.SemaphoreType.DMA
    half = lambda *s: pltpu.VMEM(s, BF16)
    full = lambda *s: pltpu.VMEM(s, F32)
    scratch = [
        half(H, rows, nodes), full(own_tiles, nodes), full(H * own_tiles, TILE), full(H * own_tiles, TILE),
        full(H * rows, k), half(H, rows, fixed_total), full(H, fixed_total, k),
        half(H, fixed_total, fixed_total), full(H * rows, k), full(H, fixed_total, k),
        full(2, H, rows, k), half(H, rows, k), half(H, rows, k), half(H, rows, k), half(H, rows, k),
        half(H, spaces, rows, k),
        full(H, fixed_total, k), half(H, fixed_total, k), half(H, times, share, k),
        full(H, share, k), full(H, spaces, share, k), half(H, fixed_total, k), half(H, fixed_total, k),
        half(H, rows, k), half(H, k, rows), full(H, xs, rows, k),
        half(H, xs, rows, k), half(H, xs, rows, k), half(H, xs, rows, k), half(H, xs, rows, k),
        full(H, rows, k), half(H, rows, k), half(H, rows, k), half(H, rows, k), half(H, rows, k),
        dma((6,)), dma((H, spaces)), dma((2,)), dma((n,)), dma((n,)), dma((n,)), dma((n,)),
        dma((n, xs)), dma((n, xs)), dma((n, spaces)),
        dma((H, times)), dma((H, times)), dma((H, spaces)), dma((H, spaces)), dma((H, times)), dma((H, times)),
        dma((H, xs)), dma((H, xs)), dma((H, xs)), dma((H, xs)),
        dma((n,)), dma((n,)), dma((n,)), dma((n,)), dma((2,)),
    ]
    anywhere = pl.BlockSpec(memory_space=pl.ANY)
    sol, fixed = pl.pallas_call(
        functools.partial(kernel, times, spaces),
        out_shape=(
            jax.ShapeDtypeStruct((H * rows, k), F32),
            jax.ShapeDtypeStruct((H, fixed_total, k), F32),
        ),
        in_specs=[anywhere] * 7,
        out_specs=(anywhere, anywhere),
        scratch_shapes=scratch,
        compiler_params=pltpu.CompilerParams(
            collective_id=0, has_side_effects=True, vmem_limit_bytes=56 * 1024 * 1024
        ),
        cost_estimate=pl.CostEstimate(
            flops=8 * H * rows * nodes * k, bytes_accessed=2 * H * rows * nodes, transcendentals=0
        ),
    )(weights, keep, rate, source, arrow, rhs, tip_factor)
    fixed_own = lax.dynamic_slice_in_dim(fixed, start, share_rows, 1)
    return sol.reshape(1, rows, H, k), fixed_own


def solution(mesh):
    placed = (
        P(None, "tm", "space", None),
        P(),
        P("tm", "space", None),
        P("tm", "space", None, None),
        P("tm", "space", None, None),
        P(None, ("tm", "space"), None),
        P(),
    )
    return jax.shard_map(
        functools.partial(on_device, mesh.shape["tm"], mesh.shape["space"]),
        mesh=mesh,
        in_specs=placed,
        out_specs=(P("tm", "space", None, None), P(None, ("tm", "space"), None)),
        check_vma=False,
    )
```

```python
import functools

import jax
import jax.numpy as jnp
from jax import lax
from jax.experimental import pallas as pl
from jax.experimental.pallas import tpu as pltpu
from jax.sharding import PartitionSpec as P

TILE = 128
CHUNKS = 4
H = 2
CORES = 2
LAG = 2
F32 = jnp.float32
BF16 = jnp.bfloat16


def turned(a):
    return a.astype(F32).T


def kernel(
    times, spaces,
    weights, keep, rate, source, arrow, rhs, tip,
    out, fixed_out,
    w_v, keep_v, table_v, rate_v, rate_p, src_v, arrow_3, arrow_v, rhs_v, tip_v, sol_v, fix_v,
    r_v, s_out, s_in, ch_out, ch_in, f_all,
    c_f, c_out, c_in1, c_part, c_in2, ff, fixed_b,
    inner, inner_t, own_part, sib_out, sib_in, red_out, red_in,
    carr, b_out, b_in, bc_out, bc_in,
    local_sem, w_sem, rate_sem, pair_s, pair_r, ch_s, ch_r,
    x_s, sib_s, f_r, c1_s, c1_r, c2_s, c2_r, c3_s, c3_r,
    sp_s, sp_r, rd_s, rd_r, bp_s, bp_r, bc_s, bc_r, out_sem,
):
    rows = f_all.shape[2]
    step_rows = rows // CHUNKS
    fixed_total = ff.shape[1]
    share = fixed_total // times
    xs = spaces // CORES
    t = lax.axis_index("tm")
    p = lax.axis_index("space")
    x = p // CORES
    c = p % CORES
    y = t % 2
    z = t // 2
    z_total = times // 2
    partner = t + 1 - 2 * y
    sibling = p + 1 - 2 * c

    def remote(src, dst, send, recv, tm, space):
        return pltpu.make_async_remote_copy(
            src_ref=src, dst_ref=dst, send_sem=send, recv_sem=recv,
            device_id={"tm": tm, "space": space}, device_id_type=pl.DeviceIdType.MESH,
        )

    loads = [
        pltpu.make_async_copy(a, b, local_sem.at[i])
        for i, (a, b) in enumerate(
            ((source, src_v), (rate, rate_v), (keep, table_v), (rhs, rhs_v), (tip, tip_v), (arrow, arrow_3))
        )
    ]
    for load in loads:
        load.start()

    def w_copy(h, q):
        cols = pl.ds(pl.multiple_of(q * rows, rows), rows)
        return pltpu.make_async_copy(weights.at[h, :, cols], w_v.at[h, :, cols], w_sem.at[h, q])

    barrier = pltpu.get_barrier_semaphore()

    def greet_t(d, _):
        pl.semaphore_signal(
            barrier, inc=1, device_id={"tm": (t + d) % times, "space": p},
            device_id_type=pl.DeviceIdType.MESH,
        )
        return 0

    def greet_s(d, _):
        pl.semaphore_signal(
            barrier, inc=1, device_id={"tm": t, "space": (p + d) % spaces},
            device_id_type=pl.DeviceIdType.MESH,
        )
        return 0

    lax.fori_loop(1, times, greet_t, 0)
    lax.fori_loop(1, spaces, greet_s, 0)
    for h in range(H):
        lax.fori_loop(0, p + 1, lambda q, _, h=h: (w_copy(h, q).start(), 0)[1], 0)
    loads[0].wait()
    loads[1].wait()

    def part(k):
        return pl.ds(pl.multiple_of(k * step_rows, step_rows), step_rows)

    def woven(h, k):
        return pl.ds(2 * k * step_rows + h, step_rows, stride=2)

    for h in range(H):
        for k in range(CHUNKS):
            s_out[h, part(k)] = src_v[woven(h, k), :].astype(BF16)
    pl.semaphore_wait(barrier, times - 1 + spaces - 1)

    def pair_copy(h, k):
        i = h * CHUNKS + k
        return remote(s_out.at[h, part(k)], s_in.at[h, part(k)], pair_s.at[i], pair_r.at[i], partner, p)

    rate_copy = remote(rate_v, rate_p, rate_sem.at[0], rate_sem.at[1], partner, p)
    rate_copy.start()
    for h in range(H):
        for k in range(CHUNKS):
            pair_copy(h, k).start()

    tiles = rows // TILE

    def spread(ref, parity):
        for h in range(H):
            for j in range(tiles):
                row = ref[pl.ds(h, 1), pl.ds(j * TILE, TILE)]
                r_v[parity, h, pl.ds(j * TILE, TILE), :] = jnp.broadcast_to(row, (TILE, TILE)).T

    spread(rate_v, y)

    @pl.when(z == 0)
    def _():
        ch_in[...] = jnp.zeros_like(ch_in)

    @pl.when(z == z_total - 1)
    def _():
        bc_in[...] = jnp.zeros_like(bc_in)

    loads[2].wait()
    tile_total = table_v.shape[0]
    own_tiles = table_v[pl.ds(pl.multiple_of(p * tiles, tiles), tiles), :]
    tile_row = p * tiles + lax.broadcasted_iota(jnp.int32, (tiles, tile_total), 0)
    tile_col = lax.broadcasted_iota(jnp.int32, (tiles, tile_total), 1)
    marks = jnp.where((own_tiles > 0) | (tile_row == tile_col), 1.0, 0.0).astype(BF16)
    hot = lax.broadcasted_iota(jnp.int32, (tile_total, tile_total * TILE), 0) == (
        lax.broadcasted_iota(jnp.int32, (tile_total, tile_total * TILE), 1) // TILE
    )
    keep_v[...] = jnp.dot(
        marks, jnp.where(hot, 1.0, 0.0).astype(BF16), preferred_element_type=F32
    )
    rate_copy.wait_recv()
    spread(rate_p, 1 - y)

    def chain_copy(h, k):
        i = h * CHUNKS + k
        return remote(
            ch_out.at[h, part(k)], ch_in.at[h, part(k)], ch_s.at[i], ch_r.at[i], (t + 2) % times, p
        )

    def x_copy(h, k, other):
        i = h * CHUNKS + k
        piece = f_all.at[h, p, part(k)]
        return remote(piece, piece, x_s.at[i, other], f_r.at[i, p], t, other * CORES + c)

    def sib_copy(h, k, from_x):
        i = h * CHUNKS + k
        q = from_x * CORES + c
        piece = f_all.at[h, q, part(k)]
        return remote(piece, piece, sib_s.at[i, from_x], f_r.at[i, q], t, sibling)

    def got(h, k, q):
        i = h * CHUNKS + k
        piece = f_all.at[h, q, part(k)]
        return remote(piece, piece, sib_s.at[i, 0], f_r.at[i, q], t, sibling)

    def scan_chunk(h, k):
        pair_copy(h, k).wait_recv()

        @pl.when(z > 0)
        def _():
            chain_copy(h, k).wait_recv()

        mine = src_v[woven(h, k), :]
        theirs = s_in[h, part(k)].astype(F32)
        s_e = jnp.where(y == 0, mine, theirs)
        s_o = jnp.where(y == 0, theirs, mine)
        f_e = s_e + r_v[0, h, part(k)] * ch_in[h, part(k)].astype(F32)
        f_o = s_o + r_v[1, h, part(k)] * f_e
        ch_out[h, part(k)] = f_o.astype(BF16)

        @pl.when(z < z_total - 1)
        def _():
            chain_copy(h, k).start()

        f_all[h, p, part(k)] = jnp.where(y == 0, f_e, f_o).astype(BF16)
        lax.fori_loop(x + 1, xs, lambda o, _: (x_copy(h, k, o).start(), 0)[1], 0)

        @pl.when(c == 0)
        def _():
            sib_copy(h, k, x).start()

    def relay(h, k):
        def one(o, _):
            got(h, k, o * CORES + c).wait_recv()
            sib_copy(h, k, o).start()
            return 0

        lax.fori_loop(0, x, one, 0)

    def ds_share(n):
        return pl.ds(pl.multiple_of(n * share, share), share)

    def c1_copy(h, d):
        to = (t + d) % times
        return remote(
            c_out.at[h, ds_share(to)], c_in1.at[h, d], c1_s.at[h, d], c1_r.at[h, d], to, p
        )

    def c2_copy(h, d):
        return remote(
            c_part.at[h], c_in2.at[h, d], c2_s.at[h, d], c2_r.at[h, d], t, (p + d) % spaces
        )

    def c3_copy(h, d):
        return remote(
            ff.at[h, ds_share(t)], ff.at[h, ds_share(t)], c3_s.at[h, d], c3_r.at[h, d],
            (t + d) % times, p,
        )

    def c3_got(h, d):
        piece = ff.at[h, ds_share((t - d + times) % times)]
        return remote(piece, piece, c3_s.at[h, d], c3_r.at[h, d], (t + d) % times, p)

    share_rows = rhs_v.shape[1]
    own_rows = pl.ds((t * spaces + p) * share_rows, share_rows)
    loads[3].wait()

    def couple(h):
        f_t = turned(f_all[h, p]).astype(BF16)
        coupling = jnp.dot(f_t, arrow_v[h], preferred_element_type=F32).T
        c_f[h] = -coupling
        c_f[h, own_rows] += rhs_v[h]
        c_out[h] = c_f[h].astype(BF16)
        lax.fori_loop(1, times, lambda d, _: (c1_copy(h, d).start(), 0)[1], 0)

    def second(h):
        def add(d, acc):
            c1_copy(h, d).wait_recv()
            return acc + c_in1[h, d].astype(F32)

        c_part[h] = lax.fori_loop(1, times, add, c_f[h, ds_share(t)])
        lax.fori_loop(1, spaces, lambda d, _: (c2_copy(h, d).start(), 0)[1], 0)

    def third(h):
        def add(d, acc):
            c2_copy(h, d).wait_recv()
            return acc + c_in2[h, d]

        ff[h, ds_share(t)] = lax.fori_loop(1, spaces, add, c_part[h]).astype(BF16)
        lax.fori_loop(1, times, lambda d, _: (c3_copy(h, d).start(), 0)[1], 0)

    def tip_solve(h):
        lax.fori_loop(1, times, lambda d, _: (c3_got(h, d).wait_recv(), 0)[1], 0)
        lower = lax.broadcasted_iota(jnp.int32, (fixed_total, fixed_total), 0) >= (
            lax.broadcasted_iota(jnp.int32, (fixed_total, fixed_total), 1)
        )
        tip_l = jnp.where(lower, tip_v[h], jnp.zeros((), BF16))
        tip_in = jnp.dot(tip_l, ff[h], preferred_element_type=F32).astype(BF16)
        fixed = jnp.dot(turned(tip_in).astype(BF16), tip_l, preferred_element_type=F32).T
        c_f[h] = fixed
        fix_v[h] = c_f[h, own_rows]
        fixed_b[h] = fixed.astype(BF16)

    block = 2 * TILE

    def masked(h, b, q):
        cols = pl.ds(pl.multiple_of(q * rows, rows), rows)
        pieces = []
        for j in range(block // TILE):
            at = pl.ds(pl.multiple_of(b * block + j * TILE, TILE), TILE)
            kept = keep_v[pl.ds(b * (block // TILE) + j, 1), cols].astype(BF16)
            pieces.append(w_v[h, at, cols] * kept)
        return jnp.concatenate(pieces, axis=0), cols

    def first_ready(h):
        def wait_block(q, _):
            w_copy(h, q).wait()
            relayed = ((q % CORES) == c) & (q // CORES < x)

            @pl.when((q < p) & jnp.logical_not(relayed))
            def _():
                lax.fori_loop(0, CHUNKS, lambda k, _: (got(h, k, q).wait_recv(), 0)[1], 0)

            return 0

        lax.fori_loop(0, p + 1, wait_block, 0)

    def first_product(h, low, high):
        def row_block(b, _):
            at = pl.ds(pl.multiple_of(b * block, block), block)

            def below(q, acc):
                piece, cols = masked(h, b, q)
                w_v[h, at, cols] = piece
                return acc + jnp.dot(piece, f_all[h, q], preferred_element_type=F32)

            acc = lax.fori_loop(0, p, below, jnp.zeros((block, f_all.shape[3]), F32))
            piece, cols = masked(h, b, p)
            row_id = b * block + lax.broadcasted_iota(jnp.int32, (block, rows), 0)
            col_id = lax.broadcasted_iota(jnp.int32, (block, rows), 1)
            piece = jnp.where(row_id >= col_id, piece, jnp.zeros((), BF16))
            w_v[h, at, cols] = piece
            acc = acc + jnp.dot(piece, f_all[h, p], preferred_element_type=F32)
            inner[h, at] = acc.astype(BF16)
            return 0

        lax.fori_loop(low, high, row_block, 0)

    def back(h, q, put):
        def col_block(b, _):
            cols = pl.ds(pl.multiple_of(q * rows + b * block, block), block)
            value = jnp.dot(inner_t[h], w_v[h, :, cols], preferred_element_type=F32).T
            put(pl.ds(pl.multiple_of(b * block, block), block), value)
            return 0

        lax.fori_loop(0, rows // block, col_block, 0)

    def sp_copy(h, o):
        return remote(sib_out.at[h, o], sib_in.at[h, o], sp_s.at[h, o], sp_r.at[h, o], t, sibling)

    def rd_copy(h, o):
        return remote(
            red_out.at[h, o], red_in.at[h, x], rd_s.at[h, o], rd_r.at[h, x], t, o * CORES + c
        )

    def rd_got(h, o):
        return remote(red_out.at[h, o], red_in.at[h, o], rd_s.at[h, o], rd_r.at[h, o], t, sibling)

    def second_product(h, low, sib_high, own_high):
        def for_sibling(o, _):
            def put(at, value):
                sib_out[h, o, at] = value.astype(BF16)

            back(h, o * CORES + 1 - c, put)
            sp_copy(h, o).start()
            return 0

        lax.fori_loop(low, sib_high, for_sibling, 0)

        def for_own(o, _):
            def put(at, value):
                own_part[h, o, at] = value

            back(h, o * CORES + c, put)
            return 0

        lax.fori_loop(low, own_high, for_own, 0)

    def pass_on(h):
        def one(o, _):
            sp_copy(h, o).wait_recv()
            red_out[h, o] = (own_part[h, o] + sib_in[h, o].astype(F32)).astype(BF16)
            rd_copy(h, o).start()
            return 0

        lax.fori_loop(0, x, one, 0)

    row_blocks = rows // block
    first_at = H * CHUNKS + LAG - row_blocks

    def scan_step(i, _):
        @pl.when(i < H * CHUNKS)
        def _():
            scan_chunk(i // CHUNKS, i % CHUNKS)

        @pl.when(i < CHUNKS)
        def _():
            at = part(i)
            for h in range(H):
                arrow_v[h, at] = arrow_3[at, h, :]

        @pl.when(i >= LAG)
        def _():
            relay((i - LAG) // CHUNKS, (i - LAG) % CHUNKS)

        for h in range(H):
            @pl.when(i == CHUNKS * (h + 1))
            def _():
                couple(h)

        @pl.when(i == first_at)
        def _():
            first_ready(0)

        @pl.when(i >= first_at)
        def _():
            first_product(0, i - first_at, i - first_at + 1)

        return 0

    loads[5].wait()
    lax.fori_loop(0, H * CHUNKS + LAG, scan_step, 0)

    def far(h):
        inner_t[h] = turned(inner[h]).astype(BF16)
        second_product(h, 0, x, x)
        pass_on(h)

    def near(h):
        second_product(h, x, x + c, x + 1)

    second(0)
    far(0)
    third(0)
    near(0)
    second(1)
    first_ready(1)
    first_product(1, 0, row_blocks)
    loads[4].wait()

    def bp_copy(h, k):
        i = h * CHUNKS + k
        return remote(b_out.at[h, part(k)], b_in.at[h, part(k)], bp_s.at[i], bp_r.at[i], partner, p)

    def bc_copy(h, k):
        i = h * CHUNKS + k
        return remote(
            bc_out.at[h, part(k)], bc_in.at[h, part(k)], bc_s.at[i], bc_r.at[i],
            (t + times - 2) % times, p,
        )

    def gather_scaled(h):
        @pl.when(c == 0)
        def _():
            sp_copy(h, x).wait_recv()

        lax.fori_loop(x + 1, xs, lambda o, _: (rd_got(h, o).wait_recv(), 0)[1], 0)

        def one(k, _):
            at = part(k)
            drop = jnp.dot(arrow_v[h, at], fixed_b[h], preferred_element_type=F32)
            carr[h, at] = own_part[h, x, at] - drop

            @pl.when(c == 0)
            def _():
                carr[h, at] += sib_in[h, x, at].astype(F32)

            def more(o, _):
                carr[h, at] += red_in[h, o, at].astype(F32)
                return 0

            lax.fori_loop(x + 1, xs, more, 0)
            b_out[h, at] = carr[h, at].astype(BF16)
            bp_copy(h, k).start()
            return 0

        lax.fori_loop(0, CHUNKS, one, 0)

    def back_chunk(h, k):
        bp_copy(h, k).wait_recv()

        @pl.when(z < z_total - 1)
        def _():
            bc_copy(h, k).wait_recv()

        mine = carr[h, part(k)]
        theirs = b_in[h, part(k)].astype(F32)
        c_e = jnp.where(y == 0, mine, theirs)
        c_o = jnp.where(y == 0, theirs, mine)
        sol_o = c_o + bc_in[h, part(k)].astype(F32)
        sol_e = c_e + r_v[1, h, part(k)] * sol_o
        bc_out[h, part(k)] = (r_v[0, h, part(k)] * sol_e).astype(BF16)

        @pl.when(z > 0)
        def _():
            bc_copy(h, k).start()

        sol_v[woven(h, k), :] = jnp.where(y == 0, sol_e, sol_o)

    tip_solve(0)
    gather_scaled(0)
    far(1)
    third(1)
    near(1)
    lax.fori_loop(0, CHUNKS, lambda k, _: (back_chunk(0, k), 0)[1], 0)
    tip_solve(1)
    gather_scaled(1)
    lax.fori_loop(0, CHUNKS, lambda k, _: (back_chunk(1, k), 0)[1], 0)
    out_copy = pltpu.make_async_copy(sol_v, out, out_sem.at[0])
    fix_copy = pltpu.make_async_copy(fix_v, fixed_out, out_sem.at[1])
    out_copy.start()
    fix_copy.start()

    rate_copy.wait_send()

    def drain(i, _):
        h, k = i // CHUNKS, i % CHUNKS
        pair_copy(h, k).wait_send()
        bp_copy(h, k).wait_send()

        @pl.when(z < z_total - 1)
        def _():
            chain_copy(h, k).wait_send()

        @pl.when(z > 0)
        def _():
            bc_copy(h, k).wait_send()

        lax.fori_loop(x + 1, xs, lambda o, _: (x_copy(h, k, o).wait_send(), 0)[1], 0)
        lax.fori_loop(0, x + 1 - c, lambda o, _: (sib_copy(h, k, o).wait_send(), 0)[1], 0)
        return 0

    lax.fori_loop(0, H * CHUNKS, drain, 0)

    for h in range(H):
        lax.fori_loop(1, times, lambda d, _, h=h: (c1_copy(h, d).wait_send(), 0)[1], 0)
        lax.fori_loop(1, spaces, lambda d, _, h=h: (c2_copy(h, d).wait_send(), 0)[1], 0)
        lax.fori_loop(1, times, lambda d, _, h=h: (c3_copy(h, d).wait_send(), 0)[1], 0)
        lax.fori_loop(0, x + c, lambda o, _, h=h: (sp_copy(h, o).wait_send(), 0)[1], 0)
        lax.fori_loop(0, x, lambda o, _, h=h: (rd_copy(h, o).wait_send(), 0)[1], 0)
    out_copy.wait()
    fix_copy.wait()


def on_device(times, spaces, inverse_factor, tile_mask, carry_rate, right_side, arrow_rows, fixed_rhs, tip_factor):
    rows = right_side.shape[1]
    nodes = inverse_factor.shape[3]
    k = right_side.shape[3]
    fixed_total = tip_factor.shape[1]
    xs = spaces // CORES
    share = fixed_total // times
    tile_total = tile_mask.shape[0]
    own_tiles = rows // TILE
    rate = carry_rate[0].T
    source = right_side.reshape(H * rows, k)
    arrow = arrow_rows[0]
    share_rows = fixed_rhs.shape[1]
    weights = inverse_factor[:, 0]
    n = H * CHUNKS
    dma = pltpu.SemaphoreType.DMA
    half = lambda *s: pltpu.VMEM(s, BF16)
    full = lambda *s: pltpu.VMEM(s, F32)
    scratch = [
        half(H, rows, nodes), full(own_tiles, nodes), pltpu.VMEM((tile_total, tile_total), jnp.int32), full(H, rows), full(H, rows),
        full(H * rows, k), half(rows, H, fixed_total), half(H, rows, fixed_total), full(H, share_rows, k),
        half(H, fixed_total, fixed_total), full(H * rows, k), full(H, share_rows, k),
        full(2, H, rows, k), half(H, rows, k), half(H, rows, k), half(H, rows, k), half(H, rows, k),
        half(H, spaces, rows, k),
        full(H, fixed_total, k), half(H, fixed_total, k), half(H, times, share, k),
        full(H, share, k), full(H, spaces, share, k), half(H, fixed_total, k), half(H, fixed_total, k),
        half(H, rows, k), half(H, k, rows), full(H, xs, rows, k),
        half(H, xs, rows, k), half(H, xs, rows, k), half(H, xs, rows, k), half(H, xs, rows, k),
        full(H, rows, k), half(H, rows, k), half(H, rows, k), half(H, rows, k), half(H, rows, k),
        dma((6,)), dma((H, spaces)), dma((2,)), dma((n,)), dma((n,)), dma((n,)), dma((n,)),
        dma((n, xs)), dma((n, xs)), dma((n, spaces)),
        dma((H, times)), dma((H, times)), dma((H, spaces)), dma((H, spaces)), dma((H, times)), dma((H, times)),
        dma((H, xs)), dma((H, xs)), dma((H, xs)), dma((H, xs)),
        dma((n,)), dma((n,)), dma((n,)), dma((n,)), dma((2,)),
    ]
    anywhere = pl.BlockSpec(memory_space=pl.ANY)
    sol, fixed = pl.pallas_call(
        functools.partial(kernel, times, spaces),
        out_shape=(
            jax.ShapeDtypeStruct((H * rows, k), F32),
            jax.ShapeDtypeStruct((H, share_rows, k), F32),
        ),
        in_specs=[anywhere] * 7,
        out_specs=(anywhere, anywhere),
        scratch_shapes=scratch,
        compiler_params=pltpu.CompilerParams(
            collective_id=0, has_side_effects=True, vmem_limit_bytes=56 * 1024 * 1024
        ),
        cost_estimate=pl.CostEstimate(
            flops=8 * H * rows * nodes * k, bytes_accessed=2 * H * rows * nodes, transcendentals=0
        ),
    )(weights, tile_mask, rate, source, arrow, fixed_rhs, tip_factor)
    return sol.reshape(1, rows, H, k), fixed


def solution(mesh):
    placed = (
        P(None, "tm", "space", None),
        P(),
        P("tm", "space", None),
        P("tm", "space", None, None),
        P("tm", "space", None, None),
        P(None, ("tm", "space"), None),
        P(),
    )
    return jax.shard_map(
        functools.partial(on_device, mesh.shape["tm"], mesh.shape["space"]),
        mesh=mesh,
        in_specs=placed,
        out_specs=(P("tm", "space", None, None), P(None, ("tm", "space"), None)),
        check_vma=False,
    )
```

```python
import functools

import jax
import jax.numpy as jnp
from jax import lax
from jax.experimental import pallas as pl
from jax.experimental.pallas import tpu as pltpu
from jax.sharding import PartitionSpec as P

TILE = 128
CHUNKS = 8
H = 2
CORES = 2
LAG = 2
F32 = jnp.float32
BF16 = jnp.bfloat16


def turned(a):
    return a.astype(F32).T


def kernel(
    times, spaces,
    weights, keep, rate, source, arrow, rhs, tip,
    out, fixed_out,
    w_v, keep_v, table_v, rate_v, rate_p, src_v, arrow_3, arrow_v, rhs_v, tip_v, sol_v, fix_v,
    r_v, s_out, s_in, ch_out, ch_in, f_all,
    c_f, c_out, c_in1, c_part, c_in2, ff, fixed_b,
    inner, inner_t, own_part, sib_out, sib_in, red_out, red_in,
    carr, b_out, b_in, bc_out, bc_in,
    local_sem, w_sem, rate_sem, pair_s, pair_r, ch_s, ch_r,
    x_s, sib_s, f_r, c1_s, c1_r, c2_s, c2_r, c3_s, c3_r,
    sp_s, sp_r, rd_s, rd_r, bp_s, bp_r, bc_s, bc_r, out_sem,
):
    rows = f_all.shape[2]
    step_rows = rows // CHUNKS
    fixed_total = ff.shape[1]
    share = fixed_total // times
    xs = spaces // CORES
    t = lax.axis_index("tm")
    p = lax.axis_index("space")
    x = p // CORES
    c = p % CORES
    y = t % 2
    z = t // 2
    z_total = times // 2
    partner = t + 1 - 2 * y
    sibling = p + 1 - 2 * c

    def remote(src, dst, send, recv, tm, space):
        return pltpu.make_async_remote_copy(
            src_ref=src, dst_ref=dst, send_sem=send, recv_sem=recv,
            device_id={"tm": tm, "space": space}, device_id_type=pl.DeviceIdType.MESH,
        )

    loads = [
        pltpu.make_async_copy(a, b, local_sem.at[i])
        for i, (a, b) in enumerate(
            ((source, src_v), (rate, rate_v), (keep, table_v), (rhs, rhs_v), (tip, tip_v), (arrow, arrow_3))
        )
    ]
    for load in loads:
        load.start()

    def w_copy(h, q):
        cols = pl.ds(pl.multiple_of(q * rows, rows), rows)
        return pltpu.make_async_copy(weights.at[h, :, cols], w_v.at[h, :, cols], w_sem.at[h, q])

    barrier = pltpu.get_barrier_semaphore()

    def greet_t(d, _):
        pl.semaphore_signal(
            barrier, inc=1, device_id={"tm": (t + d) % times, "space": p},
            device_id_type=pl.DeviceIdType.MESH,
        )
        return 0

    def greet_s(d, _):
        pl.semaphore_signal(
            barrier, inc=1, device_id={"tm": t, "space": (p + d) % spaces},
            device_id_type=pl.DeviceIdType.MESH,
        )
        return 0

    lax.fori_loop(1, times, greet_t, 0)
    lax.fori_loop(1, spaces, greet_s, 0)
    for h in range(H):
        lax.fori_loop(0, p + 1, lambda q, _, h=h: (w_copy(h, q).start(), 0)[1], 0)
    loads[0].wait()
    loads[1].wait()

    def part(k):
        return pl.ds(pl.multiple_of(k * step_rows, step_rows), step_rows)

    def woven(h, k):
        return pl.ds(2 * k * step_rows + h, step_rows, stride=2)

    for h in range(H):
        for k in range(CHUNKS):
            s_out[h, part(k)] = src_v[woven(h, k), :].astype(BF16)
    pl.semaphore_wait(barrier, times - 1 + spaces - 1)

    def pair_copy(h, k):
        i = h * CHUNKS + k
        return remote(s_out.at[h, part(k)], s_in.at[h, part(k)], pair_s.at[i], pair_r.at[i], partner, p)

    rate_copy = remote(rate_v, rate_p, rate_sem.at[0], rate_sem.at[1], partner, p)
    rate_copy.start()
    for h in range(H):
        for k in range(CHUNKS):
            pair_copy(h, k).start()

    tiles = rows // TILE

    def spread(ref, parity):
        for h in range(H):
            for j in range(tiles):
                row = ref[pl.ds(h, 1), pl.ds(j * TILE, TILE)]
                r_v[parity, h, pl.ds(j * TILE, TILE), :] = jnp.broadcast_to(row, (TILE, TILE)).T

    spread(rate_v, y)

    @pl.when(z == 0)
    def _():
        ch_in[...] = jnp.zeros_like(ch_in)

    @pl.when(z == z_total - 1)
    def _():
        bc_in[...] = jnp.zeros_like(bc_in)

    loads[2].wait()
    tile_total = table_v.shape[0]
    own_tiles = table_v[pl.ds(pl.multiple_of(p * tiles, tiles), tiles), :]
    tile_row = p * tiles + lax.broadcasted_iota(jnp.int32, (tiles, tile_total), 0)
    tile_col = lax.broadcasted_iota(jnp.int32, (tiles, tile_total), 1)
    marks = jnp.where((own_tiles > 0) | (tile_row == tile_col), 1.0, 0.0).astype(BF16)
    hot = lax.broadcasted_iota(jnp.int32, (tile_total, tile_total * TILE), 0) == (
        lax.broadcasted_iota(jnp.int32, (tile_total, tile_total * TILE), 1) // TILE
    )
    keep_v[...] = jnp.dot(
        marks, jnp.where(hot, 1.0, 0.0).astype(BF16), preferred_element_type=F32
    )
    rate_copy.wait_recv()
    spread(rate_p, 1 - y)

    def chain_copy(h, k):
        i = h * CHUNKS + k
        return remote(
            ch_out.at[h, part(k)], ch_in.at[h, part(k)], ch_s.at[i], ch_r.at[i], (t + 2) % times, p
        )

    def x_copy(h, k, other):
        i = h * CHUNKS + k
        piece = f_all.at[h, p, part(k)]
        return remote(piece, piece, x_s.at[i, other], f_r.at[i, p], t, other * CORES + c)

    def sib_copy(h, k, from_x):
        i = h * CHUNKS + k
        q = from_x * CORES + c
        piece = f_all.at[h, q, part(k)]
        return remote(piece, piece, sib_s.at[i, from_x], f_r.at[i, q], t, sibling)

    def got(h, k, q):
        i = h * CHUNKS + k
        piece = f_all.at[h, q, part(k)]
        return remote(piece, piece, sib_s.at[i, 0], f_r.at[i, q], t, sibling)

    def scan_chunk(h, k):
        pair_copy(h, k).wait_recv()

        @pl.when(z > 0)
        def _():
            chain_copy(h, k).wait_recv()

        mine = src_v[woven(h, k), :]
        theirs = s_in[h, part(k)].astype(F32)
        s_e = jnp.where(y == 0, mine, theirs)
        s_o = jnp.where(y == 0, theirs, mine)
        f_e = s_e + r_v[0, h, part(k)] * ch_in[h, part(k)].astype(F32)
        f_o = s_o + r_v[1, h, part(k)] * f_e
        ch_out[h, part(k)] = f_o.astype(BF16)

        @pl.when(z < z_total - 1)
        def _():
            chain_copy(h, k).start()

        f_all[h, p, part(k)] = jnp.where(y == 0, f_e, f_o).astype(BF16)
        lax.fori_loop(x + 1, xs, lambda o, _: (x_copy(h, k, o).start(), 0)[1], 0)

        @pl.when(c == 0)
        def _():
            sib_copy(h, k, x).start()

    def relay(h, k):
        def one(o, _):
            got(h, k, o * CORES + c).wait_recv()
            sib_copy(h, k, o).start()
            return 0

        lax.fori_loop(0, x, one, 0)

    def ds_share(n):
        return pl.ds(pl.multiple_of(n * share, share), share)

    def c1_copy(h, d):
        to = (t + d) % times
        return remote(
            c_out.at[h, ds_share(to)], c_in1.at[h, d], c1_s.at[h, d], c1_r.at[h, d], to, p
        )

    def c2_copy(h, d):
        return remote(
            c_part.at[h], c_in2.at[h, d], c2_s.at[h, d], c2_r.at[h, d], t, (p + d) % spaces
        )

    def c3_copy(h, d):
        return remote(
            ff.at[h, ds_share(t)], ff.at[h, ds_share(t)], c3_s.at[h, d], c3_r.at[h, d],
            (t + d) % times, p,
        )

    def c3_got(h, d):
        piece = ff.at[h, ds_share((t - d + times) % times)]
        return remote(piece, piece, c3_s.at[h, d], c3_r.at[h, d], (t + d) % times, p)

    share_rows = rhs_v.shape[1]
    own_rows = pl.ds((t * spaces + p) * share_rows, share_rows)
    loads[3].wait()

    def couple(h):
        f_t = turned(f_all[h, p]).astype(BF16)
        coupling = jnp.dot(f_t, arrow_v[h], preferred_element_type=F32).T
        c_f[h] = -coupling
        c_f[h, own_rows] += rhs_v[h]
        c_out[h] = c_f[h].astype(BF16)
        lax.fori_loop(1, times, lambda d, _: (c1_copy(h, d).start(), 0)[1], 0)

    def second(h):
        def add(d, acc):
            c1_copy(h, d).wait_recv()
            return acc + c_in1[h, d].astype(F32)

        c_part[h] = lax.fori_loop(1, times, add, c_f[h, ds_share(t)])
        lax.fori_loop(1, spaces, lambda d, _: (c2_copy(h, d).start(), 0)[1], 0)

    def third(h):
        def add(d, acc):
            c2_copy(h, d).wait_recv()
            return acc + c_in2[h, d]

        ff[h, ds_share(t)] = lax.fori_loop(1, spaces, add, c_part[h]).astype(BF16)
        lax.fori_loop(1, times, lambda d, _: (c3_copy(h, d).start(), 0)[1], 0)

    def tip_solve(h):
        lax.fori_loop(1, times, lambda d, _: (c3_got(h, d).wait_recv(), 0)[1], 0)
        lower = lax.broadcasted_iota(jnp.int32, (fixed_total, fixed_total), 0) >= (
            lax.broadcasted_iota(jnp.int32, (fixed_total, fixed_total), 1)
        )
        tip_l = jnp.where(lower, tip_v[h], jnp.zeros((), BF16))
        tip_in = jnp.dot(tip_l, ff[h], preferred_element_type=F32).astype(BF16)
        fixed = jnp.dot(turned(tip_in).astype(BF16), tip_l, preferred_element_type=F32).T
        c_f[h] = fixed
        fix_v[h] = c_f[h, own_rows]
        fixed_b[h] = fixed.astype(BF16)

    block = 2 * TILE

    def masked(h, b, q):
        cols = pl.ds(pl.multiple_of(q * rows, rows), rows)
        pieces = []
        for j in range(block // TILE):
            at = pl.ds(pl.multiple_of(b * block + j * TILE, TILE), TILE)
            kept = keep_v[pl.ds(b * (block // TILE) + j, 1), cols].astype(BF16)
            pieces.append(w_v[h, at, cols] * kept)
        return jnp.concatenate(pieces, axis=0), cols

    def first_ready(h):
        def wait_block(q, _):
            w_copy(h, q).wait()
            relayed = ((q % CORES) == c) & (q // CORES < x)

            @pl.when((q < p) & jnp.logical_not(relayed))
            def _():
                lax.fori_loop(0, CHUNKS, lambda k, _: (got(h, k, q).wait_recv(), 0)[1], 0)

            return 0

        lax.fori_loop(0, p + 1, wait_block, 0)

    def first_product(h, low, high):
        def row_block(b, _):
            at = pl.ds(pl.multiple_of(b * block, block), block)

            def below(q, acc):
                piece, cols = masked(h, b, q)
                w_v[h, at, cols] = piece
                return acc + jnp.dot(piece, f_all[h, q], preferred_element_type=F32)

            acc = lax.fori_loop(0, p, below, jnp.zeros((block, f_all.shape[3]), F32))
            piece, cols = masked(h, b, p)
            row_id = b * block + lax.broadcasted_iota(jnp.int32, (block, rows), 0)
            col_id = lax.broadcasted_iota(jnp.int32, (block, rows), 1)
            piece = jnp.where(row_id >= col_id, piece, jnp.zeros((), BF16))
            w_v[h, at, cols] = piece
            acc = acc + jnp.dot(piece, f_all[h, p], preferred_element_type=F32)
            inner[h, at] = acc.astype(BF16)
            return 0

        lax.fori_loop(low, high, row_block, 0)

    def back(h, q, put):
        def col_block(b, _):
            cols = pl.ds(pl.multiple_of(q * rows + b * block, block), block)
            value = jnp.dot(inner_t[h], w_v[h, :, cols], preferred_element_type=F32).T
            put(pl.ds(pl.multiple_of(b * block, block), block), value)
            return 0

        lax.fori_loop(0, rows // block, col_block, 0)

    def sp_copy(h, o):
        return remote(sib_out.at[h, o], sib_in.at[h, o], sp_s.at[h, o], sp_r.at[h, o], t, sibling)

    def rd_copy(h, o):
        return remote(
            red_out.at[h, o], red_in.at[h, x], rd_s.at[h, o], rd_r.at[h, x], t, o * CORES + c
        )

    def rd_got(h, o):
        return remote(red_out.at[h, o], red_in.at[h, o], rd_s.at[h, o], rd_r.at[h, o], t, sibling)

    def second_product(h, low, sib_high, own_high):
        def for_sibling(o, _):
            def put(at, value):
                sib_out[h, o, at] = value.astype(BF16)

            back(h, o * CORES + 1 - c, put)
            sp_copy(h, o).start()
            return 0

        lax.fori_loop(low, sib_high, for_sibling, 0)

        def for_own(o, _):
            def put(at, value):
                own_part[h, o, at] = value

            back(h, o * CORES + c, put)
            return 0

        lax.fori_loop(low, own_high, for_own, 0)

    def pass_on(h):
        def one(o, _):
            sp_copy(h, o).wait_recv()
            red_out[h, o] = (own_part[h, o] + sib_in[h, o].astype(F32)).astype(BF16)
            rd_copy(h, o).start()
            return 0

        lax.fori_loop(0, x, one, 0)

    row_blocks = rows // block
    first_at = CHUNKS + LAG

    def scan_step(i, _):
        @pl.when(i < H * CHUNKS)
        def _():
            scan_chunk(i // CHUNKS, i % CHUNKS)

        @pl.when(i < CHUNKS)
        def _():
            at = part(i)
            for h in range(H):
                arrow_v[h, at] = arrow_3[at, h, :]

        @pl.when(i >= LAG)
        def _():
            relay((i - LAG) // CHUNKS, (i - LAG) % CHUNKS)

        for h in range(H):
            @pl.when(i == CHUNKS * (h + 1))
            def _():
                couple(h)

        @pl.when(i == first_at)
        def _():
            first_ready(0)

        @pl.when((i >= first_at) & (i < first_at + row_blocks))
        def _():
            first_product(0, i - first_at, i - first_at + 1)

        return 0

    loads[5].wait()
    lax.fori_loop(0, H * CHUNKS + LAG, scan_step, 0)

    def far(h):
        inner_t[h] = turned(inner[h]).astype(BF16)
        second_product(h, 0, x, x)
        pass_on(h)

    def near(h):
        second_product(h, x, x + c, x + 1)

    second(0)
    far(0)
    third(0)
    near(0)
    second(1)
    first_ready(1)
    first_product(1, 0, row_blocks)
    loads[4].wait()

    def bp_copy(h, k):
        i = h * CHUNKS + k
        return remote(b_out.at[h, part(k)], b_in.at[h, part(k)], bp_s.at[i], bp_r.at[i], partner, p)

    def bc_copy(h, k):
        i = h * CHUNKS + k
        return remote(
            bc_out.at[h, part(k)], bc_in.at[h, part(k)], bc_s.at[i], bc_r.at[i],
            (t + times - 2) % times, p,
        )

    def gather_scaled(h):
        @pl.when(c == 0)
        def _():
            sp_copy(h, x).wait_recv()

        lax.fori_loop(x + 1, xs, lambda o, _: (rd_got(h, o).wait_recv(), 0)[1], 0)

        def one(k, _):
            at = part(k)
            drop = jnp.dot(arrow_v[h, at], fixed_b[h], preferred_element_type=F32)
            carr[h, at] = own_part[h, x, at] - drop

            @pl.when(c == 0)
            def _():
                carr[h, at] += sib_in[h, x, at].astype(F32)

            def more(o, _):
                carr[h, at] += red_in[h, o, at].astype(F32)
                return 0

            lax.fori_loop(x + 1, xs, more, 0)
            b_out[h, at] = carr[h, at].astype(BF16)
            bp_copy(h, k).start()
            return 0

        lax.fori_loop(0, CHUNKS, one, 0)

    def back_chunk(h, k):
        bp_copy(h, k).wait_recv()

        @pl.when(z < z_total - 1)
        def _():
            bc_copy(h, k).wait_recv()

        mine = carr[h, part(k)]
        theirs = b_in[h, part(k)].astype(F32)
        c_e = jnp.where(y == 0, mine, theirs)
        c_o = jnp.where(y == 0, theirs, mine)
        sol_o = c_o + bc_in[h, part(k)].astype(F32)
        sol_e = c_e + r_v[1, h, part(k)] * sol_o
        bc_out[h, part(k)] = (r_v[0, h, part(k)] * sol_e).astype(BF16)

        @pl.when(z > 0)
        def _():
            bc_copy(h, k).start()

        sol_v[woven(h, k), :] = jnp.where(y == 0, sol_e, sol_o)

    tip_solve(0)
    gather_scaled(0)
    far(1)
    third(1)
    near(1)
    lax.fori_loop(0, CHUNKS, lambda k, _: (back_chunk(0, k), 0)[1], 0)
    tip_solve(1)
    gather_scaled(1)
    lax.fori_loop(0, CHUNKS, lambda k, _: (back_chunk(1, k), 0)[1], 0)
    out_copy = pltpu.make_async_copy(sol_v, out, out_sem.at[0])
    fix_copy = pltpu.make_async_copy(fix_v, fixed_out, out_sem.at[1])
    out_copy.start()
    fix_copy.start()

    rate_copy.wait_send()

    def drain(i, _):
        h, k = i // CHUNKS, i % CHUNKS
        pair_copy(h, k).wait_send()
        bp_copy(h, k).wait_send()

        @pl.when(z < z_total - 1)
        def _():
            chain_copy(h, k).wait_send()

        @pl.when(z > 0)
        def _():
            bc_copy(h, k).wait_send()

        lax.fori_loop(x + 1, xs, lambda o, _: (x_copy(h, k, o).wait_send(), 0)[1], 0)
        lax.fori_loop(0, x + 1 - c, lambda o, _: (sib_copy(h, k, o).wait_send(), 0)[1], 0)
        return 0

    lax.fori_loop(0, H * CHUNKS, drain, 0)

    for h in range(H):
        lax.fori_loop(1, times, lambda d, _, h=h: (c1_copy(h, d).wait_send(), 0)[1], 0)
        lax.fori_loop(1, spaces, lambda d, _, h=h: (c2_copy(h, d).wait_send(), 0)[1], 0)
        lax.fori_loop(1, times, lambda d, _, h=h: (c3_copy(h, d).wait_send(), 0)[1], 0)
        lax.fori_loop(0, x + c, lambda o, _, h=h: (sp_copy(h, o).wait_send(), 0)[1], 0)
        lax.fori_loop(0, x, lambda o, _, h=h: (rd_copy(h, o).wait_send(), 0)[1], 0)
    out_copy.wait()
    fix_copy.wait()


def hand_over(sol, fixed, sol_out, fixed_out, sems):
    one = pltpu.make_async_copy(sol, sol_out, sems.at[0])
    two = pltpu.make_async_copy(fixed, fixed_out, sems.at[1])
    one.start()
    two.start()
    one.wait()
    two.wait()


def on_device(times, spaces, inverse_factor, tile_mask, carry_rate, right_side, arrow_rows, fixed_rhs, tip_factor):
    rows = right_side.shape[1]
    nodes = inverse_factor.shape[3]
    k = right_side.shape[3]
    fixed_total = tip_factor.shape[1]
    xs = spaces // CORES
    share = fixed_total // times
    tile_total = tile_mask.shape[0]
    own_tiles = rows // TILE
    rate = carry_rate[0].T
    source = right_side.reshape(H * rows, k)
    arrow = arrow_rows[0]
    share_rows = fixed_rhs.shape[1]
    weights = inverse_factor[:, 0]
    n = H * CHUNKS
    dma = pltpu.SemaphoreType.DMA
    half = lambda *s: pltpu.VMEM(s, BF16)
    full = lambda *s: pltpu.VMEM(s, F32)
    scratch = [
        half(H, rows, nodes), full(own_tiles, nodes), pltpu.VMEM((tile_total, tile_total), jnp.int32), full(H, rows), full(H, rows),
        full(H * rows, k), half(rows, H, fixed_total), half(H, rows, fixed_total), full(H, share_rows, k),
        half(H, fixed_total, fixed_total), full(H * rows, k), full(H, share_rows, k),
        full(2, H, rows, k), half(H, rows, k), half(H, rows, k), half(H, rows, k), half(H, rows, k),
        half(H, spaces, rows, k),
        full(H, fixed_total, k), half(H, fixed_total, k), half(H, times, share, k),
        full(H, share, k), full(H, spaces, share, k), half(H, fixed_total, k), half(H, fixed_total, k),
        half(H, rows, k), half(H, k, rows), full(H, xs, rows, k),
        half(H, xs, rows, k), half(H, xs, rows, k), half(H, xs, rows, k), half(H, xs, rows, k),
        full(H, rows, k), half(H, rows, k), half(H, rows, k), half(H, rows, k), half(H, rows, k),
        dma((6,)), dma((H, spaces)), dma((2,)), dma((n,)), dma((n,)), dma((n,)), dma((n,)),
        dma((n, xs)), dma((n, xs)), dma((n, spaces)),
        dma((H, times)), dma((H, times)), dma((H, spaces)), dma((H, spaces)), dma((H, times)), dma((H, times)),
        dma((H, xs)), dma((H, xs)), dma((H, xs)), dma((H, xs)),
        dma((n,)), dma((n,)), dma((n,)), dma((n,)), dma((2,)),
    ]
    anywhere = pl.BlockSpec(memory_space=pl.ANY)
    sol, fixed = pl.pallas_call(
        functools.partial(kernel, times, spaces),
        out_shape=(
            jax.ShapeDtypeStruct((H * rows, k), F32),
            jax.ShapeDtypeStruct((H, share_rows, k), F32),
        ),
        in_specs=[anywhere] * 7,
        out_specs=(anywhere, anywhere),
        scratch_shapes=scratch,
        compiler_params=pltpu.CompilerParams(
            collective_id=0, has_side_effects=True, vmem_limit_bytes=56 * 1024 * 1024
        ),
        cost_estimate=pl.CostEstimate(
            flops=8 * H * rows * nodes * k, bytes_accessed=2 * H * rows * nodes, transcendentals=0
        ),
    )(weights, tile_mask, rate, source, arrow, fixed_rhs, tip_factor)
    sol, fixed = pl.pallas_call(
        hand_over,
        out_shape=(jax.ShapeDtypeStruct(sol.shape, F32), jax.ShapeDtypeStruct(fixed.shape, F32)),
        in_specs=[anywhere] * 2,
        out_specs=(anywhere, anywhere),
        scratch_shapes=[dma((2,))],
        cost_estimate=pl.CostEstimate(flops=0, bytes_accessed=2 * sol.size * 4, transcendentals=0),
    )(sol, fixed)
    return sol.reshape(1, rows, H, k), fixed


def solution(mesh):
    placed = (
        P(None, "tm", "space", None),
        P(),
        P("tm", "space", None),
        P("tm", "space", None, None),
        P("tm", "space", None, None),
        P(None, ("tm", "space"), None),
        P(),
    )
    return jax.shard_map(
        functools.partial(on_device, mesh.shape["tm"], mesh.shape["space"]),
        mesh=mesh,
        in_specs=placed,
        out_specs=(P("tm", "space", None, None), P(None, ("tm", "space"), None)),
        check_vma=False,
    )
```

```python
import functools

import jax
import jax.numpy as jnp
from jax import lax
from jax.experimental import pallas as pl
from jax.experimental.pallas import tpu as pltpu
from jax.sharding import PartitionSpec as P

TILE = 128
CHUNKS = 8
H = 2
CORES = 2
LAG = 2
F32 = jnp.float32
BF16 = jnp.bfloat16


def turned(a):
    return a.astype(F32).T


def kernel(
    times, spaces,
    weights, keep, rate, source, arrow, rhs, tip,
    out, fixed_out,
    w_v, keep_v, table_v, rate_v, rate_p, src_v, arrow_3, arrow_v, rhs_v, tip_v, sol_v, fix_v,
    r_v, s_out, s_in, ch_out, ch_in, f_all,
    c_f, c_out, c_in1, c_part, c_in2, ff, fixed_b,
    inner, inner_t, own_part, sib_out, sib_in, red_out, red_in,
    carr, b_out, b_in, bc_out, bc_in,
    local_sem, w_sem, rate_sem, pair_s, pair_r, ch_s, ch_r,
    x_s, sib_s, f_r, c1_s, c1_r, c2_s, c2_r, c3_s, c3_r,
    sp_s, sp_r, rd_s, rd_r, bp_s, bp_r, bc_s, bc_r, out_sem,
):
    rows = f_all.shape[2]
    step_rows = rows // CHUNKS
    fixed_total = ff.shape[1]
    share = fixed_total // times
    xs = spaces // CORES
    t = lax.axis_index("tm")
    p = lax.axis_index("space")
    x = p // CORES
    c = p % CORES
    y = t % 2
    z = t // 2
    z_total = times // 2
    partner = t + 1 - 2 * y
    sibling = p + 1 - 2 * c

    def remote(src, dst, send, recv, tm, space):
        return pltpu.make_async_remote_copy(
            src_ref=src, dst_ref=dst, send_sem=send, recv_sem=recv,
            device_id={"tm": tm, "space": space}, device_id_type=pl.DeviceIdType.MESH,
        )

    loads = [
        pltpu.make_async_copy(a, b, local_sem.at[i])
        for i, (a, b) in enumerate(
            ((source, src_v), (rate, rate_v), (keep, table_v), (rhs, rhs_v), (tip, tip_v), (arrow, arrow_3))
        )
    ]
    for load in loads:
        load.start()

    def w_copy(h, q):
        cols = pl.ds(pl.multiple_of(q * rows, rows), rows)
        return pltpu.make_async_copy(weights.at[h, :, cols], w_v.at[h, :, cols], w_sem.at[h, q])

    barrier = pltpu.get_barrier_semaphore()

    def greet_t(d, _):
        pl.semaphore_signal(
            barrier, inc=1, device_id={"tm": (t + d) % times, "space": p},
            device_id_type=pl.DeviceIdType.MESH,
        )
        return 0

    def greet_s(d, _):
        pl.semaphore_signal(
            barrier, inc=1, device_id={"tm": t, "space": (p + d) % spaces},
            device_id_type=pl.DeviceIdType.MESH,
        )
        return 0

    lax.fori_loop(1, times, greet_t, 0)
    lax.fori_loop(1, spaces, greet_s, 0)
    for h in range(H):
        lax.fori_loop(0, p + 1, lambda q, _, h=h: (w_copy(h, q).start(), 0)[1], 0)
    loads[0].wait()
    loads[1].wait()

    def part(k):
        return pl.ds(pl.multiple_of(k * step_rows, step_rows), step_rows)

    def woven(h, k):
        return pl.ds(2 * k * step_rows + h, step_rows, stride=2)

    for h in range(H):
        for k in range(CHUNKS):
            s_out[h, part(k)] = src_v[woven(h, k), :].astype(BF16)
    pl.semaphore_wait(barrier, times - 1 + spaces - 1)

    def pair_copy(h, k):
        i = h * CHUNKS + k
        return remote(s_out.at[h, part(k)], s_in.at[h, part(k)], pair_s.at[i], pair_r.at[i], partner, p)

    rate_copy = remote(rate_v, rate_p, rate_sem.at[0], rate_sem.at[1], partner, p)
    rate_copy.start()
    for h in range(H):
        for k in range(CHUNKS):
            pair_copy(h, k).start()

    tiles = rows // TILE

    def spread(ref, parity):
        for h in range(H):
            for j in range(tiles):
                row = ref[pl.ds(h, 1), pl.ds(j * TILE, TILE)]
                r_v[parity, h, pl.ds(j * TILE, TILE), :] = jnp.broadcast_to(row, (TILE, TILE)).T

    spread(rate_v, y)

    @pl.when(z == 0)
    def _():
        ch_in[...] = jnp.zeros_like(ch_in)

    @pl.when(z == z_total - 1)
    def _():
        bc_in[...] = jnp.zeros_like(bc_in)

    loads[2].wait()
    tile_total = table_v.shape[0]
    own_tiles = table_v[pl.ds(pl.multiple_of(p * tiles, tiles), tiles), :]
    tile_row = p * tiles + lax.broadcasted_iota(jnp.int32, (tiles, tile_total), 0)
    tile_col = lax.broadcasted_iota(jnp.int32, (tiles, tile_total), 1)
    marks = jnp.where((own_tiles > 0) | (tile_row == tile_col), 1.0, 0.0).astype(BF16)
    hot = lax.broadcasted_iota(jnp.int32, (tile_total, tile_total * TILE), 0) == (
        lax.broadcasted_iota(jnp.int32, (tile_total, tile_total * TILE), 1) // TILE
    )
    keep_v[...] = jnp.dot(
        marks, jnp.where(hot, 1.0, 0.0).astype(BF16), preferred_element_type=F32
    )
    rate_copy.wait_recv()
    spread(rate_p, 1 - y)

    def chain_copy(h, k):
        i = h * CHUNKS + k
        return remote(
            ch_out.at[h, part(k)], ch_in.at[h, part(k)], ch_s.at[i], ch_r.at[i], (t + 2) % times, p
        )

    def x_copy(h, k, other):
        i = h * CHUNKS + k
        piece = f_all.at[h, p, part(k)]
        return remote(piece, piece, x_s.at[i, other], f_r.at[i, p], t, other * CORES + c)

    def sib_copy(h, k, from_x):
        i = h * CHUNKS + k
        q = from_x * CORES + c
        piece = f_all.at[h, q, part(k)]
        return remote(piece, piece, sib_s.at[i, from_x], f_r.at[i, q], t, sibling)

    def got(h, k, q):
        i = h * CHUNKS + k
        piece = f_all.at[h, q, part(k)]
        return remote(piece, piece, sib_s.at[i, 0], f_r.at[i, q], t, sibling)

    def scan_chunk(h, k):
        pair_copy(h, k).wait_recv()

        @pl.when(z > 0)
        def _():
            chain_copy(h, k).wait_recv()

        mine = src_v[woven(h, k), :]
        theirs = s_in[h, part(k)].astype(F32)
        s_e = jnp.where(y == 0, mine, theirs)
        s_o = jnp.where(y == 0, theirs, mine)
        f_e = s_e + r_v[0, h, part(k)] * ch_in[h, part(k)].astype(F32)
        f_o = s_o + r_v[1, h, part(k)] * f_e
        ch_out[h, part(k)] = f_o.astype(BF16)

        @pl.when(z < z_total - 1)
        def _():
            chain_copy(h, k).start()

        f_all[h, p, part(k)] = jnp.where(y == 0, f_e, f_o).astype(BF16)
        lax.fori_loop(x + 1, xs, lambda o, _: (x_copy(h, k, o).start(), 0)[1], 0)

        @pl.when(c == 0)
        def _():
            sib_copy(h, k, x).start()

    def relay(h, k):
        def one(o, _):
            got(h, k, o * CORES + c).wait_recv()
            sib_copy(h, k, o).start()
            return 0

        lax.fori_loop(0, x, one, 0)

    def ds_share(n):
        return pl.ds(pl.multiple_of(n * share, share), share)

    def c1_copy(h, d):
        to = (t + d) % times
        return remote(
            c_out.at[h, ds_share(to)], c_in1.at[h, d], c1_s.at[h, d], c1_r.at[h, d], to, p
        )

    def c2_copy(h, d):
        return remote(
            c_part.at[h], c_in2.at[h, d], c2_s.at[h, d], c2_r.at[h, d], t, (p + d) % spaces
        )

    def c3_copy(h, d):
        return remote(
            ff.at[h, ds_share(t)], ff.at[h, ds_share(t)], c3_s.at[h, d], c3_r.at[h, d],
            (t + d) % times, p,
        )

    def c3_got(h, d):
        piece = ff.at[h, ds_share((t - d + times) % times)]
        return remote(piece, piece, c3_s.at[h, d], c3_r.at[h, d], (t + d) % times, p)

    share_rows = rhs_v.shape[1]
    own_rows = pl.ds((t * spaces + p) * share_rows, share_rows)
    loads[3].wait()

    def couple(h):
        f_t = turned(f_all[h, p]).astype(BF16)
        coupling = jnp.dot(f_t, arrow_v[h], preferred_element_type=F32).T
        c_f[h] = -coupling
        c_f[h, own_rows] += rhs_v[h]
        c_out[h] = c_f[h].astype(BF16)
        lax.fori_loop(1, times, lambda d, _: (c1_copy(h, d).start(), 0)[1], 0)

    def second(h):
        def add(d, acc):
            c1_copy(h, d).wait_recv()
            return acc + c_in1[h, d].astype(F32)

        c_part[h] = lax.fori_loop(1, times, add, c_f[h, ds_share(t)])
        lax.fori_loop(1, spaces, lambda d, _: (c2_copy(h, d).start(), 0)[1], 0)

    def third(h):
        def add(d, acc):
            c2_copy(h, d).wait_recv()
            return acc + c_in2[h, d]

        ff[h, ds_share(t)] = lax.fori_loop(1, spaces, add, c_part[h]).astype(BF16)
        lax.fori_loop(1, times, lambda d, _: (c3_copy(h, d).start(), 0)[1], 0)

    def tip_solve(h):
        lax.fori_loop(1, times, lambda d, _: (c3_got(h, d).wait_recv(), 0)[1], 0)
        lower = lax.broadcasted_iota(jnp.int32, (fixed_total, fixed_total), 0) >= (
            lax.broadcasted_iota(jnp.int32, (fixed_total, fixed_total), 1)
        )
        tip_l = jnp.where(lower, tip_v[h], jnp.zeros((), BF16))
        tip_in = jnp.dot(tip_l, ff[h], preferred_element_type=F32).astype(BF16)
        fixed = jnp.dot(turned(tip_in).astype(BF16), tip_l, preferred_element_type=F32).T
        c_f[h] = fixed
        fix_v[h] = c_f[h, own_rows]
        fixed_b[h] = fixed.astype(BF16)

    block = 2 * TILE

    def masked(h, b, q):
        cols = pl.ds(pl.multiple_of(q * rows, rows), rows)
        pieces = []
        for j in range(block // TILE):
            at = pl.ds(pl.multiple_of(b * block + j * TILE, TILE), TILE)
            kept = keep_v[pl.ds(b * (block // TILE) + j, 1), cols].astype(BF16)
            pieces.append(w_v[h, at, cols] * kept)
        return jnp.concatenate(pieces, axis=0), cols

    def first_ready(h):
        def wait_block(q, _):
            w_copy(h, q).wait()
            relayed = ((q % CORES) == c) & (q // CORES < x)

            @pl.when((q < p) & jnp.logical_not(relayed))
            def _():
                lax.fori_loop(0, CHUNKS, lambda k, _: (got(h, k, q).wait_recv(), 0)[1], 0)

            return 0

        lax.fori_loop(0, p + 1, wait_block, 0)

    def first_product(h, low, high):
        def row_block(b, _):
            at = pl.ds(pl.multiple_of(b * block, block), block)

            def below(q, acc):
                piece, cols = masked(h, b, q)
                w_v[h, at, cols] = piece
                return acc + jnp.dot(piece, f_all[h, q], preferred_element_type=F32)

            acc = lax.fori_loop(0, p, below, jnp.zeros((block, f_all.shape[3]), F32))
            piece, cols = masked(h, b, p)
            row_id = b * block + lax.broadcasted_iota(jnp.int32, (block, rows), 0)
            col_id = lax.broadcasted_iota(jnp.int32, (block, rows), 1)
            piece = jnp.where(row_id >= col_id, piece, jnp.zeros((), BF16))
            w_v[h, at, cols] = piece
            acc = acc + jnp.dot(piece, f_all[h, p], preferred_element_type=F32)
            inner[h, at] = acc.astype(BF16)
            return 0

        lax.fori_loop(low, high, row_block, 0)

    row_blocks = rows // block

    def span(b):
        return pl.ds(pl.multiple_of(b * block, block), block)

    def back(h, q, b):
        cols = pl.ds(pl.multiple_of(q * rows + b * block, block), block)
        return jnp.dot(inner_t[h], w_v[h, :, cols], preferred_element_type=F32).T

    def sp_copy(h, o, b):
        n = o * row_blocks + b
        return remote(
            sib_out.at[h, o, span(b)], sib_in.at[h, o, span(b)], sp_s.at[h, n], sp_r.at[h, n], t, sibling
        )

    def rd_copy(h, o, b):
        return remote(
            red_out.at[h, o, span(b)], red_in.at[h, x, span(b)], rd_s.at[h, o * row_blocks + b],
            rd_r.at[h, x * row_blocks + b], t, o * CORES + c,
        )

    def rd_got(h, o, b):
        n = o * row_blocks + b
        return remote(
            red_out.at[h, o, span(b)], red_in.at[h, o, span(b)], rd_s.at[h, n], rd_r.at[h, n], t, sibling
        )

    def for_sibling(h, o, b):
        sib_out[h, o, span(b)] = back(h, o * CORES + 1 - c, b).astype(BF16)
        sp_copy(h, o, b).start()

    def for_own(h, o, b):
        own_part[h, o, span(b)] = back(h, o * CORES + c, b)

    def pass_on(h, o, b):
        sp_copy(h, o, b).wait_recv()
        total = own_part[h, o, span(b)] + sib_in[h, o, span(b)].astype(F32)
        red_out[h, o, span(b)] = total.astype(BF16)
        rd_copy(h, o, b).start()

    first_at = CHUNKS + LAG

    def scan_step(i, _):
        @pl.when(i < H * CHUNKS)
        def _():
            scan_chunk(i // CHUNKS, i % CHUNKS)

        @pl.when(i < CHUNKS)
        def _():
            at = part(i)
            for h in range(H):
                arrow_v[h, at] = arrow_3[at, h, :]

        @pl.when(i >= LAG)
        def _():
            relay((i - LAG) // CHUNKS, (i - LAG) % CHUNKS)

        for h in range(H):
            @pl.when(i == CHUNKS * (h + 1))
            def _():
                couple(h)

        @pl.when(i == first_at)
        def _():
            first_ready(0)

        @pl.when((i >= first_at) & (i < first_at + row_blocks))
        def _():
            first_product(0, i - first_at, i - first_at + 1)

        return 0

    loads[5].wait()
    lax.fori_loop(0, H * CHUNKS + LAG, scan_step, 0)

    def far(h):
        inner_t[h] = turned(inner[h]).astype(BF16)
        count = x * row_blocks

        def one(i, _):
            @pl.when(i < count)
            def _():
                for_sibling(h, i // row_blocks, i % row_blocks)
                for_own(h, i // row_blocks, i % row_blocks)

            @pl.when(i >= 1)
            def _():
                pass_on(h, (i - 1) // row_blocks, (i - 1) % row_blocks)

            return 0

        lax.fori_loop(0, count + jnp.minimum(x, 1), one, 0)

    def near(h):
        def one(b, _):
            @pl.when(c == 1)
            def _():
                for_sibling(h, x, b)

            for_own(h, x, b)
            return 0

        lax.fori_loop(0, row_blocks, one, 0)

    second(0)
    far(0)
    third(0)
    near(0)
    second(1)
    first_ready(1)
    first_product(1, 0, row_blocks)
    loads[4].wait()

    def bp_copy(h, k):
        i = h * CHUNKS + k
        return remote(b_out.at[h, part(k)], b_in.at[h, part(k)], bp_s.at[i], bp_r.at[i], partner, p)

    def bc_copy(h, k):
        i = h * CHUNKS + k
        return remote(
            bc_out.at[h, part(k)], bc_in.at[h, part(k)], bc_s.at[i], bc_r.at[i],
            (t + times - 2) % times, p,
        )

    def gather_scaled(h):
        per = CHUNKS // row_blocks

        def one(k, _):
            at = part(k)

            @pl.when(k % per == 0)
            def _():
                @pl.when(c == 0)
                def _():
                    sp_copy(h, x, k // per).wait_recv()

                lax.fori_loop(x + 1, xs, lambda o, _: (rd_got(h, o, k // per).wait_recv(), 0)[1], 0)

            drop = jnp.dot(arrow_v[h, at], fixed_b[h], preferred_element_type=F32)
            carr[h, at] = own_part[h, x, at] - drop

            @pl.when(c == 0)
            def _():
                carr[h, at] += sib_in[h, x, at].astype(F32)

            def more(o, _):
                carr[h, at] += red_in[h, o, at].astype(F32)
                return 0

            lax.fori_loop(x + 1, xs, more, 0)
            b_out[h, at] = carr[h, at].astype(BF16)
            bp_copy(h, k).start()
            return 0

        lax.fori_loop(0, CHUNKS, one, 0)

    def back_chunk(h, k):
        bp_copy(h, k).wait_recv()

        @pl.when(z < z_total - 1)
        def _():
            bc_copy(h, k).wait_recv()

        mine = carr[h, part(k)]
        theirs = b_in[h, part(k)].astype(F32)
        c_e = jnp.where(y == 0, mine, theirs)
        c_o = jnp.where(y == 0, theirs, mine)
        sol_o = c_o + bc_in[h, part(k)].astype(F32)
        sol_e = c_e + r_v[1, h, part(k)] * sol_o
        bc_out[h, part(k)] = (r_v[0, h, part(k)] * sol_e).astype(BF16)

        @pl.when(z > 0)
        def _():
            bc_copy(h, k).start()

        sol_v[woven(h, k), :] = jnp.where(y == 0, sol_e, sol_o)

    tip_solve(0)
    gather_scaled(0)
    far(1)
    third(1)
    near(1)
    lax.fori_loop(0, CHUNKS, lambda k, _: (back_chunk(0, k), 0)[1], 0)
    tip_solve(1)
    gather_scaled(1)
    lax.fori_loop(0, CHUNKS, lambda k, _: (back_chunk(1, k), 0)[1], 0)
    out_copy = pltpu.make_async_copy(sol_v, out, out_sem.at[0])
    fix_copy = pltpu.make_async_copy(fix_v, fixed_out, out_sem.at[1])
    out_copy.start()
    fix_copy.start()

    rate_copy.wait_send()

    def drain(i, _):
        h, k = i // CHUNKS, i % CHUNKS
        pair_copy(h, k).wait_send()
        bp_copy(h, k).wait_send()

        @pl.when(z < z_total - 1)
        def _():
            chain_copy(h, k).wait_send()

        @pl.when(z > 0)
        def _():
            bc_copy(h, k).wait_send()

        lax.fori_loop(x + 1, xs, lambda o, _: (x_copy(h, k, o).wait_send(), 0)[1], 0)
        lax.fori_loop(0, x + 1 - c, lambda o, _: (sib_copy(h, k, o).wait_send(), 0)[1], 0)
        return 0

    lax.fori_loop(0, H * CHUNKS, drain, 0)

    for h in range(H):
        lax.fori_loop(1, times, lambda d, _, h=h: (c1_copy(h, d).wait_send(), 0)[1], 0)
        lax.fori_loop(1, spaces, lambda d, _, h=h: (c2_copy(h, d).wait_send(), 0)[1], 0)
        lax.fori_loop(1, times, lambda d, _, h=h: (c3_copy(h, d).wait_send(), 0)[1], 0)
        lax.fori_loop(
            0, (x + c) * row_blocks,
            lambda i, _, h=h: (sp_copy(h, i // row_blocks, i % row_blocks).wait_send(), 0)[1], 0,
        )
        lax.fori_loop(
            0, x * row_blocks,
            lambda i, _, h=h: (rd_copy(h, i // row_blocks, i % row_blocks).wait_send(), 0)[1], 0,
        )
    out_copy.wait()
    fix_copy.wait()


def hand_over(sol, fixed, sol_out, fixed_out):
    sol_out[...] = sol[...]
    fixed_out[...] = fixed[...]


def on_device(times, spaces, inverse_factor, tile_mask, carry_rate, right_side, arrow_rows, fixed_rhs, tip_factor):
    rows = right_side.shape[1]
    nodes = inverse_factor.shape[3]
    k = right_side.shape[3]
    fixed_total = tip_factor.shape[1]
    xs = spaces // CORES
    share = fixed_total // times
    tile_total = tile_mask.shape[0]
    own_tiles = rows // TILE
    rate = carry_rate[0].T
    source = right_side.reshape(H * rows, k)
    arrow = arrow_rows[0]
    share_rows = fixed_rhs.shape[1]
    weights = inverse_factor[:, 0]
    n = H * CHUNKS
    dma = pltpu.SemaphoreType.DMA
    half = lambda *s: pltpu.VMEM(s, BF16)
    full = lambda *s: pltpu.VMEM(s, F32)
    scratch = [
        half(H, rows, nodes), full(own_tiles, nodes), pltpu.VMEM((tile_total, tile_total), jnp.int32), full(H, rows), full(H, rows),
        full(H * rows, k), half(rows, H, fixed_total), half(H, rows, fixed_total), full(H, share_rows, k),
        half(H, fixed_total, fixed_total), full(H * rows, k), full(H, share_rows, k),
        full(2, H, rows, k), half(H, rows, k), half(H, rows, k), half(H, rows, k), half(H, rows, k),
        half(H, spaces, rows, k),
        full(H, fixed_total, k), half(H, fixed_total, k), half(H, times, share, k),
        full(H, share, k), full(H, spaces, share, k), half(H, fixed_total, k), half(H, fixed_total, k),
        half(H, rows, k), half(H, k, rows), full(H, xs, rows, k),
        half(H, xs, rows, k), half(H, xs, rows, k), half(H, xs, rows, k), half(H, xs, rows, k),
        full(H, rows, k), half(H, rows, k), half(H, rows, k), half(H, rows, k), half(H, rows, k),
        dma((6,)), dma((H, spaces)), dma((2,)), dma((n,)), dma((n,)), dma((n,)), dma((n,)),
        dma((n, xs)), dma((n, xs)), dma((n, spaces)),
        dma((H, times)), dma((H, times)), dma((H, spaces)), dma((H, spaces)), dma((H, times)), dma((H, times)),
        *[dma((H, xs * rows // (2 * TILE)))] * 4,
        dma((n,)), dma((n,)), dma((n,)), dma((n,)), dma((2,)),
    ]
    anywhere = pl.BlockSpec(memory_space=pl.ANY)
    sol, fixed = pl.pallas_call(
        functools.partial(kernel, times, spaces),
        out_shape=(
            jax.ShapeDtypeStruct((H * rows, k), F32),
            jax.ShapeDtypeStruct((H, share_rows, k), F32),
        ),
        in_specs=[anywhere] * 7,
        out_specs=(anywhere, anywhere),
        scratch_shapes=scratch,
        compiler_params=pltpu.CompilerParams(
            collective_id=0, has_side_effects=True, vmem_limit_bytes=56 * 1024 * 1024
        ),
        cost_estimate=pl.CostEstimate(
            flops=8 * H * rows * nodes * k, bytes_accessed=2 * H * rows * nodes, transcendentals=0
        ),
    )(weights, tile_mask, rate, source, arrow, fixed_rhs, tip_factor)
    sol, fixed = pl.pallas_call(
        hand_over,
        out_shape=(jax.ShapeDtypeStruct(sol.shape, F32), jax.ShapeDtypeStruct(fixed.shape, F32)),
        grid=(2,),
        in_specs=[
            pl.BlockSpec((sol.shape[0] // 2, k), lambda i: (i, 0)),
            pl.BlockSpec((1,) + fixed.shape[1:], lambda i: (i, 0, 0)),
        ],
        out_specs=(
            pl.BlockSpec((sol.shape[0] // 2, k), lambda i: (i, 0)),
            pl.BlockSpec((1,) + fixed.shape[1:], lambda i: (i, 0, 0)),
        ),
        cost_estimate=pl.CostEstimate(flops=0, bytes_accessed=2 * sol.size * 4, transcendentals=0),
    )(sol, fixed)
    return sol.reshape(1, rows, H, k), fixed


def solution(mesh):
    placed = (
        P(None, "tm", "space", None),
        P(),
        P("tm", "space", None),
        P("tm", "space", None, None),
        P("tm", "space", None, None),
        P(None, ("tm", "space"), None),
        P(),
    )
    return jax.shard_map(
        functools.partial(on_device, mesh.shape["tm"], mesh.shape["space"]),
        mesh=mesh,
        in_specs=placed,
        out_specs=(P("tm", "space", None, None), P(None, ("tm", "space"), None)),
        check_vma=False,
    )
```
